256 devices in a mesh: ctx: 8 (over y, core), exp: 32 (over z, x).
Axes of the slice: x: 4, y: 4, z: 8, core: 2. Of those that a mesh axis runs over, the one named last changes fastest.
Arguments:
- moe_rows: bfloat16 [8192, 7168], P('exp', 'ctx'), may hold values from -6 to 6
- expert_ids: int32 [8192, 4], P('exp'), may hold values from 0 to 31, all different within a row; in each aligned block of 256 rows (0 to 255, 256 to 511, ...) at most 41 rows name the same one
- route_weight: float32 [8192, 4], P('exp'), may hold values from 0.2 to 1
- w_gate: bfloat16 [32, 7168, 2048], P('exp', 'ctx'), may hold values from -0.0625 to 0.0625
- w_up: bfloat16 [32, 7168, 2048], P('exp', 'ctx'), may hold values from -0.0625 to 0.0625
- w_down: bfloat16 [32, 2048, 7168], P('exp', None, 'ctx'), may hold values from -0.125 to 0.125
Outputs:
- mixed_rows: bfloat16 [8192, 7168], P('exp', 'ctx')
The draws below stay inside these ranges and needn't reach their ends.
Inputs may be any that keep to these rules, and one draw needn't show every extreme that they name: `expert_ids`: the 4 experts of a token differ. In each aligned block of 256 rows (the expert tokens of one index of exp) no expert is chosen by more than 41 rows, a bound that some block reaches.
All inputs are finite; a program needn't handle non-finite values.
Results may differ from the reference program's by a relative error of at most 0.029.
Values may be sent and summed in bfloat16 or wider, within the bound.
No kernel may reach another device: no remote copies, remote signals or barrier semaphores. Data moves between devices by JAX's collectives and lax.ppermute only.
A program may use at most 128 MiB of HBM per device.

```python
import math
import jax
import jax.numpy as jnp
import numpy as np
from jax import lax

D = 7168
HIDDEN_SIZE = 2048
TOP = 4
MOE_GROUP = 256
MOE_TOKENS = 8192
EXPERTS = 32
CAP = 41
N_CTX = 8
N_EXP = 32


def level_of(stream_key, extent, cuts, smallest, high):
    level = 1.0
    for dim, shards_of in cuts:
        steps = jax.random.uniform(jax.random.fold_in(jax.random.fold_in(stream_key, 6), dim), (shards_of,), jnp.float32, smallest / len(cuts), high / len(cuts))
        level = level * jnp.repeat(jnp.exp(steps), extent[dim] // shards_of).reshape((-1,) + (1,) * (len(extent) - 1 - dim))
    return level


def deal_out(own_key, own, number, rows, amount, top, limit, skew):
    order = jax.random.permutation(own_key, amount)
    crowded, usual = load_shares(amount, rows * top, limit, skew, True), load_shares(amount, rows * top, limit, skew, False)
    places = jnp.arange(amount)

    def named(tallies, offset_by):
        used = int((tallies > 0).sum())
        fixed = max(1, used // 4)
        passed = fixed + (places - fixed + offset_by * (used - fixed)) % max(1, amount - fixed)
        return jnp.zeros((amount,), jnp.int32).at[order[jnp.where(places < fixed, places, passed)]].set(jnp.asarray(tallies, jnp.int32))

    tallies = jnp.where(number % 4 == 0, named(crowded, number // 4), named(usual, number - number // 4 - 1))
    mixed = jax.random.permutation(jax.random.fold_in(own, 3), amount)
    donor, taker = mixed[0:amount // 2 * 2:2], mixed[1:amount // 2 * 2:2]
    slack = jnp.minimum(tallies[donor] - 1, limit - tallies[taker]) // 2
    slack = jnp.where((donor == order[0]) | (taker == order[0]) | (tallies[taker] == 0), 0, jnp.maximum(slack, 0))
    passed = jax.random.randint(jax.random.fold_in(own, 4), (amount // 2,), 0, 1 << 20) % (slack + 1)
    tallies = tallies.at[donor].add(-passed).at[taker].add(passed)
    members = jnp.searchsorted(jnp.cumsum(tallies), jnp.arange(rows * top), side="right").astype(jnp.int32)
    grid = members.reshape(top, rows).T
    grid = grid[jax.random.permutation(jax.random.fold_in(own, 1), rows)]
    offset_by = jax.random.randint(jax.random.fold_in(own, 2), (rows, 1), 0, top)
    return jnp.take_along_axis(grid, (jnp.arange(top)[None, :] + offset_by) % top, axis=1)


def load_shares(amount, total, most, slope, full):
    loads = [(1 << 20) // math.isqrt(grade ** slope) + 1 for grade in range(1, amount + 1)]
    largest = most if full else min(most, max(-(-total // amount), total * loads[0] // sum(loads)))
    least = 1 if total - largest >= amount - 1 else 0
    given, spare = [largest] + [least] * (amount - 1), total - largest - least * (amount - 1)
    while spare > 0:
        movable = [i for i in range(1, amount) if given[i] < largest] or [i for i in range(1, amount) if given[i] < most]
        mass, left = sum([loads[i] for i in movable]), spare
        for i in movable:
            more = min(most - given[i], max(1, left * loads[i] // mass), spare)
            given[i] = given[i] + more
            spare = spare - more
    return np.array(given)


def scatter_about(own_key, shape, scale, limit, cuts=(), held_as=jnp.bfloat16):
    result = scale * jax.random.normal(own_key, shape, jnp.float32)
    if cuts:
        result = result * level_of(own_key, shape, cuts, -0.22, 0.18)
    return jnp.clip(result, -limit, limit).astype(held_as)


def setup_inputs(seed: int = 0) -> dict:
    seeds = jax.random.split(jax.random.key(seed), 7)
    moe_rows = scatter_about(seeds[0], (MOE_TOKENS, D), 1.0, 6.0, ((0, 32), (1, 8)))
    expert_ids_keys = jax.random.split(jax.random.fold_in(seeds[1], 1), MOE_TOKENS // MOE_GROUP)
    expert_ids_turns = jax.random.permutation(jax.random.fold_in(seeds[1], 3), MOE_TOKENS // MOE_GROUP)
    expert_ids = jax.vmap(lambda own, number: deal_out(jax.random.fold_in(seeds[1], 2), own, number, MOE_GROUP, EXPERTS, TOP, CAP, 2))(expert_ids_keys, expert_ids_turns).reshape((MOE_TOKENS, TOP))
    route_weight = jnp.clip(0.2 + 0.8 * jax.random.uniform(seeds[2], (MOE_TOKENS, TOP), jnp.float32) ** level_of(seeds[2], (MOE_TOKENS, TOP), ((0, 32),), -0.2, 0.2), 0.2, 1.0)
    w_gate = scatter_about(seeds[3], (EXPERTS, D, HIDDEN_SIZE), D ** -0.5, 0.0625, ((0, 32), (1, 8)))
    w_up = scatter_about(seeds[4], (EXPERTS, D, HIDDEN_SIZE), D ** -0.5, 0.0625, ((0, 32), (1, 8)))
    w_down = scatter_about(seeds[5], (EXPERTS, HIDDEN_SIZE, D), HIDDEN_SIZE ** -0.5, 0.125, ((0, 32), (2, 8)))
    return dict(moe_rows=moe_rows, expert_ids=expert_ids, route_weight=route_weight, w_gate=w_gate, w_up=w_up, w_down=w_down)


def expert_block(rows, gate_w, up_w, down_w):
    row_count = rows.shape[0]
    width = D // N_CTX
    pieces = rows.reshape(row_count, N_CTX, width).astype(jnp.float32)
    gate_parts = jnp.einsum("rcd,cdh->crh", pieces, gate_w.reshape(N_CTX, width, HIDDEN_SIZE).astype(jnp.float32))
    up_parts = jnp.einsum("rcd,cdh->crh", pieces, up_w.reshape(N_CTX, width, HIDDEN_SIZE).astype(jnp.float32))
    gate_sum = jnp.sum(lax.optimization_barrier(gate_parts.astype(jnp.bfloat16)).astype(jnp.float32), axis=0)
    up_sum = jnp.sum(lax.optimization_barrier(up_parts.astype(jnp.bfloat16)).astype(jnp.float32), axis=0)
    active = (jax.nn.silu(gate_sum) * up_sum).astype(jnp.bfloat16)
    return jnp.dot(active, down_w, preferred_element_type=jnp.float32).astype(jnp.bfloat16)


def reference(moe_rows, expert_ids, route_weight, w_gate, w_up, w_down):
    total_rows = moe_rows.shape[0]
    item_count = total_rows * TOP
    max_rows = N_EXP * CAP
    chosen = expert_ids.reshape(item_count).astype(jnp.int32)
    sorted_ids = jnp.argsort(chosen, stable=True).astype(jnp.int32)
    onehot = (chosen[:, None] == jnp.arange(EXPERTS, dtype=jnp.int32)[None, :]).astype(jnp.int32)
    counts = jnp.sum(onehot, axis=0).astype(jnp.int32)
    starts = (jnp.cumsum(counts) - counts).astype(jnp.int32)
    padded_order = jnp.concatenate([(sorted_ids // TOP).astype(jnp.int32), jnp.full((max_rows,), total_rows, jnp.int32)])
    padded_rows = jnp.concatenate([moe_rows, jnp.zeros((1, D), jnp.bfloat16)], 0)

    def per_expert(expert_index):
        picked = lax.dynamic_slice_in_dim(padded_order, starts[expert_index], max_rows)
        live_rows = jnp.arange(max_rows, dtype=jnp.int32) < counts[expert_index]
        picked = jnp.where(live_rows, picked, total_rows).astype(jnp.int32)
        return expert_block(padded_rows[picked], w_gate[expert_index], w_up[expert_index], w_down[expert_index])

    results = lax.map(per_expert, jnp.arange(EXPERTS, dtype=jnp.int32))
    inverse = jnp.zeros((item_count,), jnp.int32).at[sorted_ids].set(jnp.arange(item_count, dtype=jnp.int32))
    rank_rows = (inverse - starts[chosen]).astype(jnp.int32)
    routed = results[chosen, rank_rows].reshape(total_rows, TOP, D)
    mixed_rows = jnp.sum(route_weight[:, :, None] * routed.astype(jnp.float32), axis=1).astype(jnp.bfloat16)
    return mixed_rows
```

```python
import functools

import jax
import jax.numpy as jnp
from jax import lax
from jax.experimental import pallas as pl
from jax.experimental.pallas import tpu as pltpu
from jax.sharding import Mesh, PartitionSpec as P

BF16 = jnp.bfloat16
F32 = jnp.float32

NY, NZ, NX = 4, 8, 4
TOKENS = 256
TOP = 4
CAP = 41
META = 16
CHUNKS = ((0, -1, 1, -2, 2), (-3, 3, 4))
VMEM = 48 * 1024 * 1024


def rows_of(chunk):
    return -(-len(chunk) * CAP // 16) * 16


def shift(value, axis, size, step):
    return lax.ppermute(value, axis, [(i, (i + step) % size) for i in range(size)])


def cost(flops, moved):
    return pl.CostEstimate(flops=flops, bytes_accessed=moved, transcendentals=0)


def params(grid_rank=0):
    if grid_rank:
        return pltpu.CompilerParams(
            vmem_limit_bytes=VMEM, dimension_semantics=("arbitrary",) * grid_rank
        )
    return pltpu.CompilerParams(vmem_limit_bytes=VMEM)


def whole():
    return pl.BlockSpec(memory_space=pltpu.VMEM)


def scalars():
    return pl.BlockSpec(memory_space=pltpu.SMEM)


def pack_kernel(rows_ref, ids_ref, weight_ref, out_ref):
    out_ref[0:TOKENS, :] = rows_ref[...]
    both = jnp.concatenate([ids_ref[...].astype(F32), weight_ref[...]], axis=1)
    meta = jnp.concatenate([both.T, jnp.zeros((META - 2 * TOP, TOKENS), F32)], axis=0)
    tail = jnp.zeros((META, out_ref.shape[1] - TOKENS), BF16)
    out_ref[TOKENS : TOKENS + META, :] = jnp.concatenate([meta.astype(BF16), tail], axis=1)


def pack(rows, ids, weight):
    width = rows.shape[1]
    return pl.pallas_call(
        pack_kernel,
        out_shape=jax.ShapeDtypeStruct((TOKENS + META, width), BF16),
        in_specs=[whole()] * 3,
        out_specs=whole(),
        compiler_params=params(),
        cost_estimate=cost(0, 4 * TOKENS * width),
    )(rows, ids, weight)


def places(meta, place_ref):
    z, x = place_ref[0], place_ref[1]
    ids = meta[0:TOP, :]
    weight = meta[TOP : 2 * TOP, :]
    hit, scale = [], []
    for j in range(NX):
        expert = (z * NX + lax.rem(x + j, NX)).astype(F32)
        same = (ids == expert).astype(F32)
        hit.append(jnp.sum(same, axis=0, keepdims=True))
        scale.append(jnp.sum(same * weight, axis=0, keepdims=True))
    hit, scale = jnp.concatenate(hit, axis=0), jnp.concatenate(scale, axis=0)
    before = (
        lax.broadcasted_iota(jnp.int32, (TOKENS, TOKENS), 0)
        <= lax.broadcasted_iota(jnp.int32, (TOKENS, TOKENS), 1)
    ).astype(F32).astype(BF16)
    padded = jnp.concatenate([hit, jnp.zeros_like(hit)], axis=0).astype(BF16)
    rank = jnp.dot(padded, before, preferred_element_type=F32)[0:NX] - 1.0
    return hit, rank, scale


def dispatch_kernel(chunk, place_ref, *refs):
    rows = rows_of(chunk)
    count = len(chunk)
    out_refs, meta_ref = refs[-NX - 3 : -3], refs[-3]
    picked, held = refs[-2:]
    blocks = refs[: -NX - 3]
    taken = 0
    index = lax.broadcasted_iota(jnp.int32, (rows, TOKENS), 0).astype(F32)
    for i, offset in enumerate(chunk):
        if offset == 4:
            first, second = blocks[taken : taken + 2]
            taken += 2
            half = first.shape[0]
            held[i * TOKENS : i * TOKENS + half, :] = first[...]
            held[i * TOKENS + half : (i + 1) * TOKENS, :] = second[0 : TOKENS - half, :]
            meta = second[TOKENS - half : TOKENS - half + META, 0:TOKENS]
        else:
            block = blocks[taken]
            taken += 1
            held[i * TOKENS : (i + 1) * TOKENS, :] = block[0:TOKENS, :]
            meta = block[TOKENS : TOKENS + META, 0:TOKENS]
        meta_ref[i * META : (i + 1) * META, :] = meta
        hit, rank, _ = places(meta.astype(F32), place_ref)
        slot = jnp.where(hit > 0, rank + float(CAP * i), -1.0)
        for j in range(NX):
            picked[j * rows : (j + 1) * rows, i * TOKENS : (i + 1) * TOKENS] = (
                (index == slot[j : j + 1, :]).astype(F32).astype(BF16)
            )
    for j in range(NX):
        out_refs[j][...] = jnp.dot(
            picked[j * rows : (j + 1) * rows, :], held[...], preferred_element_type=F32
        ).astype(BF16)


def dispatch(chunk, place, blocks):
    rows, count, width = rows_of(chunk), len(chunk), blocks[0].shape[1]
    return pl.pallas_call(
        functools.partial(dispatch_kernel, chunk),
        out_shape=[jax.ShapeDtypeStruct((rows, width), BF16)] * NX
        + [jax.ShapeDtypeStruct((count * META, TOKENS), BF16)],
        in_specs=[scalars()] + [whole()] * len(blocks),
        out_specs=[whole()] * (NX + 1),
        scratch_shapes=[
            pltpu.VMEM((NX * rows, count * TOKENS), BF16),
            pltpu.VMEM((count * TOKENS, width), BF16),
        ],
        compiler_params=params(),
        cost_estimate=cost(
            2 * NX * rows * count * TOKENS * width, 4 * NX * rows * width + 2 * count * TOKENS * width
        ),
    )(place, *blocks)


def combine_kernel(chunk, place_ref, meta_ref, *refs):
    rows = rows_of(chunk)
    out_refs = refs[NX : NX + len(chunk)]
    held = refs[-1]
    for j in range(NX):
        held[j * rows : (j + 1) * rows, :] = refs[j][...]
    index = lax.broadcasted_iota(jnp.int32, (TOKENS, NX * rows), 1).astype(F32)
    for i in range(len(chunk)):
        meta = meta_ref[i * META : (i + 1) * META, :].astype(F32)
        hit, rank, scale = places(meta, place_ref)
        start = lax.broadcasted_iota(jnp.int32, (NX, TOKENS), 0).astype(F32) * float(rows)
        slot = jnp.where(hit > 0, rank + start + float(CAP * i), -1.0)
        both = jnp.concatenate([slot, scale], axis=0).T
        mix = jnp.zeros((TOKENS, NX * rows), F32)
        for j in range(NX):
            mix = jnp.where(index == both[:, j : j + 1], both[:, NX + j : NX + j + 1], mix)
        out_refs[i][...] = jnp.dot(
            mix.astype(BF16), held[...], preferred_element_type=F32
        ).astype(BF16)


def combine(chunk, place, meta, returned):
    rows, count, width = rows_of(chunk), len(chunk), returned[0].shape[1]
    return pl.pallas_call(
        functools.partial(combine_kernel, chunk),
        out_shape=[jax.ShapeDtypeStruct((TOKENS, width), BF16)] * count,
        in_specs=[scalars()] + [whole()] * (NX + 1),
        out_specs=[whole()] * count,
        scratch_shapes=[pltpu.VMEM((NX * rows, width), BF16)],
        compiler_params=params(),
        cost_estimate=cost(
            2 * NX * rows * count * TOKENS * width, 2 * NX * rows * width + 2 * count * TOKENS * width
        ),
    )(place, meta, *returned)


def up_kernel(place_ref, *refs):
    blocks, (gate_ref, up_ref, out_ref, held) = refs[:NX], refs[NX:]
    rows = blocks[0].shape[0]

    @pl.when(pl.program_id(0) == 0)
    def _():
        for j in range(NX):
            held[j * rows : (j + 1) * rows, :] = blocks[j][...]

    part = gate_ref.shape[2]
    out_ref[0, :, 0:part] = jnp.dot(
        held[...], gate_ref[0], preferred_element_type=F32
    ).astype(BF16)
    out_ref[0, :, part : 2 * part] = jnp.dot(
        held[...], up_ref[0], preferred_element_type=F32
    ).astype(BF16)


def up_projection(place, blocks, w_gate, w_up):
    rows, width = blocks[0].shape
    hidden = w_gate.shape[2]
    part = hidden // (2 * NY)
    total = NX * rows

    def weight_block(k, place_ref):
        return (0, 0, lax.rem(place_ref[0] + k, NY) * 2 + place_ref[1])

    def fixed(k, place_ref):
        return (0, 0)

    return pl.pallas_call(
        up_kernel,
        out_shape=jax.ShapeDtypeStruct((NY, total, 2 * part), BF16),
        grid_spec=pltpu.PrefetchScalarGridSpec(
            num_scalar_prefetch=1,
            grid=(NY,),
            in_specs=[pl.BlockSpec((rows, width), fixed)] * NX
            + [pl.BlockSpec((1, width, part), weight_block)] * 2,
            out_specs=pl.BlockSpec((1, total, 2 * part), lambda k, place_ref: (k, 0, 0)),
            scratch_shapes=[pltpu.VMEM((total, width), BF16)],
        ),
        compiler_params=params(1),
        cost_estimate=cost(2 * total * width * hidden, 2 * (total * (width + hidden) + width * hidden)),
    )(place, *blocks, w_gate, w_up)


def down_kernel(count, place_ref, *refs):
    actives, weight_refs, out_refs, held = (
        refs[: 2 * count],
        refs[2 * count : 2 * count + 2 * NY],
        refs[2 * count + 2 * NY : -1],
        refs[-1],
    )
    part = weight_refs[0].shape[1]
    for c in range(2):
        for i in range(count):
            block = actives[c * count + i]
            if i < NY - 1:
                held[:, (c * NY + i) * part : (c * NY + i + 1) * part] = block[...]
            else:
                half = block.shape[0]
                start = (i - NY + 1) * half
                held[start : start + half, (c * NY + NY - 1) * part : (c * NY + NY) * part] = block[...]
    weight = jnp.concatenate([w[0] for w in weight_refs], axis=0)
    rows = out_refs[0].shape[0]
    for j in range(NX):
        out_refs[j][...] = jnp.dot(
            held[j * rows : (j + 1) * rows, :], weight, preferred_element_type=F32
        ).astype(BF16)


def down_projection(place, own, other, w_down):
    total, part = own[0].shape
    width = w_down.shape[2]
    count = len(own)

    def weight_block(distance, flip):
        def at(k, place_ref):
            core = place_ref[1] if not flip else 1 - place_ref[1]
            return (0, lax.rem(place_ref[0] + distance, NY) * 2 + core, 0)

        return pl.BlockSpec((1, part, width), at)

    def fixed(k, place_ref):
        return (0, 0)

    rows = total // NX
    actives = list(own) + list(other)
    order = (0, NY - 1, 1, 2)
    return pl.pallas_call(
        functools.partial(down_kernel, count),
        out_shape=[jax.ShapeDtypeStruct((rows, width), BF16)] * NX,
        grid_spec=pltpu.PrefetchScalarGridSpec(
            num_scalar_prefetch=1,
            grid=(1,),
            in_specs=[pl.BlockSpec(a.shape, fixed) for a in actives]
            + [weight_block(d, flip) for flip in (False, True) for d in order],
            out_specs=[pl.BlockSpec((rows, width), fixed)] * NX,
            scratch_shapes=[pltpu.VMEM((total, 2 * NY * part), BF16)],
        ),
        compiler_params=params(1),
        cost_estimate=cost(
            4 * total * NY * part * width, 2 * (total * (2 * NY * part + width) + 2 * NY * part * width)
        ),
    )(place, *actives, *([w_down] * (2 * NY)))


def total_of(*terms):
    return sum(t.astype(F32) for t in terms).astype(BF16)


def per_device(moe_rows, expert_ids, route_weight, w_gate, w_up, w_down):
    y, core = lax.axis_index("y"), lax.axis_index("core")
    z, x = lax.axis_index("z"), lax.axis_index("x")
    place_zx = jnp.stack([z, x]).astype(jnp.int32)
    place_own = jnp.stack([y, core]).astype(jnp.int32)
    place_other = jnp.stack([y, 1 - core]).astype(jnp.int32)

    own = pack(moe_rows, expert_ids, route_weight)
    arrived = {0: (own,)}
    plus, minus = own, own
    for step in range(1, NZ // 2):
        plus, minus = shift(plus, "z", NZ, 1), shift(minus, "z", NZ, -1)
        arrived[-step], arrived[step] = (plus,), (minus,)
    half = TOKENS // 2
    arrived[NZ // 2] = (
        shift(plus[:half], "z", NZ, 1),
        shift(minus[half:], "z", NZ, -1),
    )

    sums = {}
    for chunk in CHUNKS:
        blocks = [b for offset in chunk for b in arrived[offset]]
        *outgoing, meta = dispatch(chunk, place_zx, blocks)
        incoming = [outgoing[0]] + [shift(outgoing[j], "x", NX, j) for j in range(1, NX)]
        sent = up_projection(place_other, incoming, w_gate, w_up)
        got = lax.ppermute(sent, "core", [(0, 1), (1, 0)])
        kept = up_projection(place_own, incoming, w_gate, w_up)
        middle = kept.shape[1] // 2
        part = kept.shape[2] // 2
        far_plus = shift(total_of(kept[2, :middle], got[2, :middle]), "y", NY, 1)
        far_minus = shift(total_of(kept[2, middle:], got[2, middle:]), "y", NY, -1)
        near_plus = jnp.concatenate(
            [total_of(kept[1, :middle], got[1, :middle], far_plus), total_of(kept[1, middle:], got[1, middle:])]
        )
        near_minus = jnp.concatenate(
            [total_of(kept[3, :middle], got[3, :middle]), total_of(kept[3, middle:], got[3, middle:], far_minus)]
        )
        near_plus, near_minus = shift(near_plus, "y", NY, 1), shift(near_minus, "y", NY, -1)
        both = sum(t.astype(F32) for t in (kept[0], got[0], near_plus, near_minus))
        active = (jax.nn.silu(both[:, :part]) * both[:, part:]).astype(BF16)
        below, above = shift(active, "y", NY, 1), shift(active, "y", NY, -1)
        mine = [
            active,
            below,
            above,
            shift(below[:middle], "y", NY, 1),
            shift(above[middle:], "y", NY, -1),
        ]
        other = [lax.ppermute(m, "core", [(0, 1), (1, 0)]) for m in mine]
        results = down_projection(place_own, mine, other, w_down)
        returned = [results[0]] + [shift(results[j], "x", NX, -j) for j in range(1, NX)]
        for offset, partial in zip(chunk, combine(chunk, place_zx, meta, returned), strict=True):
            sums[offset] = partial

    far = sums[NZ // 2]
    plus, minus = shift(far[:half], "z", NZ, 1), shift(far[half:], "z", NZ, -1)
    plus = jnp.concatenate([total_of(sums[3][:half], plus), sums[3][half:]])
    minus = jnp.concatenate([sums[-3][:half], total_of(sums[-3][half:], minus)])
    for step in (2, 1):
        plus = total_of(sums[step], shift(plus, "z", NZ, 1))
        minus = total_of(sums[-step], shift(minus, "z", NZ, -1))
    return total_of(sums[0], shift(plus, "z", NZ, 1), shift(minus, "z", NZ, -1))


def solution(mesh):
    split = Mesh(mesh.devices.reshape(NY, 2, NZ, NX), ("y", "core", "z", "x"))
    exp, ctx = ("z", "x"), ("y", "core")
    return jax.shard_map(
        per_device,
        mesh=split,
        in_specs=(
            P(exp, ctx),
            P(exp, None),
            P(exp, None),
            P(exp, ctx, None),
            P(exp, ctx, None),
            P(exp, None, ctx),
        ),
        out_specs=P(exp, ctx),
        check_vma=False,
    )
```

```python
import functools

import jax
import jax.numpy as jnp
from jax import lax
from jax.experimental import pallas as pl
from jax.experimental.pallas import tpu as pltpu
from jax.sharding import Mesh, PartitionSpec as P

BF16 = jnp.bfloat16
F32 = jnp.float32

NY, NZ, NX = 4, 8, 4
TOKENS = 256
TOP = 4
CAP = 41
META = 16
CHUNKS = ((0, -1, 1, -2, 2), (-3, 3, 4))
ORDER = (
    ("pick", 0),
    ("join", 0),
    ("pick", 1),
    ("far", 0),
    ("rest", 0),
    ("add", 0),
    ("join", 1),
    ("far", 1),
    ("rest", 1),
    ("act", 0),
    ("add", 1),
    ("act", 1),
    ("down", 1),
    ("down", 0),
    ("mix", 1),
    ("mix", 0),
)
VMEM = 22 * 1024 * 1024
WORK = 20_000_000_000
TOKEN = jax.ShapeDtypeStruct((8, 128), jnp.float32)


def rows_of(chunk):
    return -(-len(chunk) * CAP // 16) * 16


def lanes_of(chunk):
    return -(-rows_of(chunk) // 128) * 128


def shift(value, axis, size, step):
    return lax.ppermute(value, axis, [(i, (i + step) % size) for i in range(size)])


def swap(value):
    return lax.ppermute(value, "core", [(0, 1), (1, 0)])


def whole():
    return pl.BlockSpec(memory_space=pltpu.VMEM)


def shaped(*shape):
    return jax.ShapeDtypeStruct(shape, BF16)


def run(kernel, after, place, operands, outs, scratch=(), grid=None, in_specs=None):
    in_specs = in_specs or [whole()] * len(operands)

    def body(place_ref, *refs):
        refs = refs[len(after) :]
        token_ref = refs[len(operands)]
        token_ref[...] = jnp.zeros_like(token_ref)
        kernel(place_ref, *refs[: len(operands)], *refs[len(operands) + 1 :])

    outs = [TOKEN] + list(outs)
    return pl.pallas_call(
        body,
        out_shape=outs,
        grid_spec=pltpu.PrefetchScalarGridSpec(
            num_scalar_prefetch=1,
            grid=grid or (1,),
            in_specs=[whole()] * len(after) + list(in_specs),
            out_specs=[pl.BlockSpec(o.shape, lambda *_, n=len(o.shape): (0,) * n) for o in outs],
            scratch_shapes=list(scratch),
        ),
        compiler_params=pltpu.CompilerParams(
            vmem_limit_bytes=VMEM, dimension_semantics=("arbitrary",) * len(grid or (1,))
        ),
        cost_estimate=pl.CostEstimate(flops=WORK, bytes_accessed=1, transcendentals=0),
    )(place, *after, *operands)


def pack_kernel(rows_ref, ids_ref, weight_ref, out_ref, ids, weight, sems):
    copies = [
        pltpu.make_async_copy(rows_ref, out_ref.at[pl.ds(0, TOKENS)], sems.at[0]),
        pltpu.make_async_copy(ids_ref, ids, sems.at[1]),
        pltpu.make_async_copy(weight_ref, weight, sems.at[2]),
    ]
    for copy in copies:
        copy.start()
    copies[1].wait()
    copies[2].wait()
    blank = jnp.zeros((META - 2 * TOP, TOKENS), F32)
    meta = jnp.concatenate([ids[...].astype(F32), weight[...], blank], axis=0)
    tail = jnp.zeros((META, out_ref.shape[1] - TOKENS), BF16)
    out_ref[TOKENS : TOKENS + META, :] = jnp.concatenate([meta.astype(BF16), tail], axis=1)
    copies[0].wait()


def pack(rows, ids, weight):
    return pl.pallas_call(
        pack_kernel,
        out_shape=shaped(TOKENS + META, rows.shape[1]),
        in_specs=[pl.BlockSpec(memory_space=pltpu.HBM)] * 3,
        out_specs=whole(),
        scratch_shapes=[
            pltpu.VMEM(ids.shape, ids.dtype),
            pltpu.VMEM(weight.shape, weight.dtype),
            pltpu.SemaphoreType.DMA((3,)),
        ],
        compiler_params=pltpu.CompilerParams(vmem_limit_bytes=VMEM),
    )(rows, ids, weight)


def halves_kernel(place_ref, gate_ref, up_ref, out_ref):
    half = gate_ref.shape[2]
    out_ref[:, 0:half] = gate_ref[0]
    out_ref[:, half : 2 * half] = up_ref[0]


def other_half(after, place, w_gate, w_up):
    _, width, hidden = w_gate.shape

    def block(k, place_ref):
        return (0, 0, 1 - place_ref[3])

    spec = pl.BlockSpec((1, width, hidden // 2), block)
    return run(
        halves_kernel, after, place, [w_gate, w_up], [shaped(width, hidden)], in_specs=[spec, spec]
    )


def places(meta, place_ref):
    ids = meta[0:TOP, :]
    weight = meta[TOP : 2 * TOP, :]
    hit, scale = [], []
    for j in range(NX):
        expert = place_ref[0] * NX + lax.rem(place_ref[1] + j, NX)
        same = (ids == expert.astype(F32)).astype(F32)
        hit.append(jnp.sum(same, axis=0, keepdims=True))
        scale.append(jnp.sum(same * weight, axis=0, keepdims=True))
    hit, scale = jnp.concatenate(hit, axis=0), jnp.concatenate(scale, axis=0)
    before = (
        lax.broadcasted_iota(jnp.int32, (TOKENS, TOKENS), 0)
        <= lax.broadcasted_iota(jnp.int32, (TOKENS, TOKENS), 1)
    ).astype(F32).astype(BF16)
    padded = jnp.concatenate([hit, jnp.zeros_like(hit)], axis=0).astype(BF16)
    rank = jnp.dot(padded, before, preferred_element_type=F32)[0:NX] - 1.0
    return hit, rank, scale


def pick_kernel(chunk, place_ref, *refs):
    rows = rows_of(chunk)
    blocks, out_refs, (meta_ref, picked, held) = refs[: -NX - 3], refs[-NX - 3 : -3], refs[-3:]
    taken = 0
    index = lax.broadcasted_iota(jnp.int32, (rows, TOKENS), 0).astype(F32)
    for i, offset in enumerate(chunk):
        if offset == NZ // 2:
            first, second = blocks[taken : taken + 2]
            taken += 2
            half = first.shape[0]
            held[i * TOKENS : i * TOKENS + half, :] = first[...]
            held[i * TOKENS + half : (i + 1) * TOKENS, :] = second[0 : TOKENS - half, :]
            meta = second[TOKENS - half : TOKENS - half + META, 0:TOKENS]
        else:
            block = blocks[taken]
            taken += 1
            held[i * TOKENS : (i + 1) * TOKENS, :] = block[0:TOKENS, :]
            meta = block[TOKENS : TOKENS + META, 0:TOKENS]
        meta_ref[i * META : (i + 1) * META, :] = meta
        hit, rank, _ = places(meta.astype(F32), place_ref)
        slot = jnp.where(hit > 0, rank + float(CAP * i), -1.0)
        for j in range(NX):
            picked[j * rows : (j + 1) * rows, i * TOKENS : (i + 1) * TOKENS] = (
                (index == slot[j : j + 1, :]).astype(F32).astype(BF16)
            )
    found = jnp.dot(picked[...], held[...], preferred_element_type=F32).astype(BF16)
    for j in range(NX):
        out_refs[j][...] = found[j * rows : (j + 1) * rows, :]


def pick(chunk, after, place, blocks):
    rows, count, width = rows_of(chunk), len(chunk), blocks[0].shape[1]
    return run(
        functools.partial(pick_kernel, chunk),
        after,
        place,
        blocks,
        [shaped(rows, width)] * NX + [shaped(count * META, TOKENS)],
        [pltpu.VMEM((NX * rows, count * TOKENS), BF16), pltpu.VMEM((count * TOKENS, width), BF16)],
    )


def mix_kernel(chunk, place_ref, meta_ref, *refs):
    rows, lanes = rows_of(chunk), lanes_of(chunk)
    returned, out_refs, (mixed, held) = refs[:NX], refs[NX:-2], refs[-2:]
    width = held.shape[1]
    for j in range(NX):
        held[j * lanes : j * lanes + rows, :] = returned[j][...]
        if lanes > rows:
            held[j * lanes + rows : (j + 1) * lanes, :] = jnp.zeros((lanes - rows, width), BF16)
    index = lax.broadcasted_iota(jnp.int32, (TOKENS, lanes), 1).astype(F32)
    for i in range(len(chunk)):
        meta = meta_ref[i * META : (i + 1) * META, :].astype(F32)
        hit, rank, scale = places(meta, place_ref)
        slot = jnp.where(hit > 0, rank + float(CAP * i), -1.0)
        both = jnp.concatenate([slot, scale], axis=0).T
        for j in range(NX):
            mixed[i * TOKENS : (i + 1) * TOKENS, j * lanes : (j + 1) * lanes] = jnp.where(
                index == both[:, j : j + 1], both[:, NX + j : NX + j + 1], 0.0
            ).astype(BF16)
    total = jnp.dot(mixed[...], held[...], preferred_element_type=F32).astype(BF16)
    for i in range(len(chunk)):
        out_refs[i][...] = total[i * TOKENS : (i + 1) * TOKENS, :]


def mix(chunk, after, place, meta, returned):
    lanes, count, width = lanes_of(chunk), len(chunk), returned[0].shape[1]
    return run(
        functools.partial(mix_kernel, chunk),
        after,
        place,
        [meta, *returned],
        [shaped(TOKENS, width)] * count,
        [pltpu.VMEM((count * TOKENS, NX * lanes), BF16), pltpu.VMEM((NX * lanes, width), BF16)],
    )


def join_kernel(place_ref, *refs):
    rows = refs[0].shape[0]
    for j in range(NX):
        refs[NX][j * rows : (j + 1) * rows, :] = refs[j][...]


def up_kernel(place_ref, *refs):
    own, other, gate_ref, up_ref, gate2_ref, up2_ref = refs[:6]
    out_refs, held = refs[6:-1], refs[-1]
    width = own.shape[1]
    part = gate_ref.shape[2]

    @pl.when(pl.program_id(0) == 0)
    def _():
        held[:, 0:width] = own[...]
        held[:, width : 2 * width] = other[...]

    gate = jnp.dot(
        held[...], jnp.concatenate([gate_ref[0], gate2_ref[...]], axis=0), preferred_element_type=F32
    ).astype(BF16)
    up = jnp.dot(
        held[...], jnp.concatenate([up_ref[0], up2_ref[...]], axis=0), preferred_element_type=F32
    ).astype(BF16)
    if len(out_refs) == 2:
        half = out_refs[0].shape[0]
        for k in range(2):
            out_refs[k][:, 0:part] = gate[k * half : (k + 1) * half]
            out_refs[k][:, part : 2 * part] = up[k * half : (k + 1) * half]
    else:
        for k, out_ref in enumerate(out_refs):

            @pl.when(pl.program_id(0) == k)
            def _(out_ref=out_ref):
                out_ref[:, 0:part] = gate
                out_ref[:, part : 2 * part] = up


def up_projection(first, count, after, place, own, other, weights):
    w_gate, w_up, swapped = weights
    total, width = own.shape
    part = w_gate.shape[2] // (2 * NY)

    def column(k, place_ref):
        return lax.rem(place_ref[2] + first + k, NY)

    def own_block(k, place_ref):
        return (0, 0, place_ref[3] * NY + column(k, place_ref))

    def gate_block(k, place_ref):
        return (0, column(k, place_ref))

    def up_block(k, place_ref):
        return (0, NY + column(k, place_ref))

    outs = [shaped(total, 2 * part)] * count if count > 1 else [shaped(total // 2, 2 * part)] * 2
    return run(
        up_kernel,
        after,
        place,
        [own, other, w_gate, w_up, swapped, swapped],
        outs,
        [pltpu.VMEM((total, 2 * width), BF16)],
        (count,),
        [whole()] * 2
        + [pl.BlockSpec((1, width, part), own_block)] * 2
        + [pl.BlockSpec((width, part), gate_block), pl.BlockSpec((width, part), up_block)],
    )


def add_kernel(place_ref, plus_ref, minus_ref, far_plus, far_minus, out_plus, out_minus):
    half = far_plus.shape[0]
    out_plus[0:half] = (plus_ref[0:half].astype(F32) + far_plus[...].astype(F32)).astype(BF16)
    out_plus[half:] = plus_ref[half:]
    out_minus[0:half] = minus_ref[0:half]
    out_minus[half:] = (minus_ref[half:].astype(F32) + far_minus[...].astype(F32)).astype(BF16)


def act_kernel(place_ref, own, plus, minus, out_ref):
    total = own[...].astype(F32) + plus[...].astype(F32) + minus[...].astype(F32)
    part = out_ref.shape[1]
    out_ref[...] = (jax.nn.silu(total[:, 0:part]) * total[:, part : 2 * part]).astype(BF16)


def down_kernel(count, place_ref, *refs):
    actives, weight_refs, out_refs, held = (
        refs[: 2 * count],
        refs[2 * count : 2 * count + 2 * NY],
        refs[2 * count + 2 * NY : -1],
        refs[-1],
    )
    part = weight_refs[0].shape[1]
    for c in range(2):
        for i in range(count):
            block = actives[c * count + i]
            if i < NY - 1:
                held[:, (c * NY + i) * part : (c * NY + i + 1) * part] = block[...]
            else:
                half = block.shape[0]
                start = (i - NY + 1) * half
                held[start : start + half, (c * NY + NY - 1) * part : (c * NY + NY) * part] = block[...]
    weight = jnp.concatenate([w[0] for w in weight_refs], axis=0)
    rows = out_refs[0].shape[0]
    result = jnp.dot(held[...], weight, preferred_element_type=F32).astype(BF16)
    for j in range(NX):
        out_refs[j][...] = result[j * rows : (j + 1) * rows, :]


def down_projection(after, place, own, other, w_down):
    total, part = own[0].shape
    width = w_down.shape[2]

    def weight_block(distance, flip):
        def at(k, place_ref):
            core = 1 - place_ref[3] if flip else place_ref[3]
            return (0, core * NY + lax.rem(place_ref[2] + distance, NY), 0)

        return pl.BlockSpec((1, part, width), at)

    actives = list(own) + list(other)
    return run(
        functools.partial(down_kernel, len(own)),
        after,
        place,
        actives + [w_down] * (2 * NY),
        [shaped(total // NX, width)] * NX,
        [pltpu.VMEM((total, 2 * NY * part), BF16)],
        None,
        [whole()] * len(actives)
        + [weight_block(d, flip) for flip in (False, True) for d in (0, NY - 1, 1, 2)],
    )


def total_of(*terms):
    return sum(t.astype(F32) for t in terms).astype(BF16)


def across_x(values, way):
    return [values[0]] + [shift(values[j], "x", NX, way * j) for j in range(1, NX)]


def per_device(moe_rows, expert_ids, route_weight, w_gate, w_up, w_down):
    place = jnp.stack([lax.axis_index(a) for a in ("z", "x", "y", "core")]).astype(jnp.int32)

    own = pack(moe_rows, expert_ids.T, route_weight.T)
    arrived = {0: (own,)}
    plus, minus = own, own
    for step in range(1, NZ // 2):
        plus, minus = shift(plus, "z", NZ, 1), shift(minus, "z", NZ, -1)
        arrived[-step], arrived[step] = (plus,), (minus,)
    last, swapped = other_half([], place, w_gate, w_up)
    weights = (w_gate, w_up, swap(swapped))
    half = TOKENS // 2
    arrived[NZ // 2] = (
        shift(plus[:half], "z", NZ, 1),
        shift(minus[half:], "z", NZ, -1),
    )

    state = [{} for _ in CHUNKS]
    sums = {}
    for step, c in ORDER:
        chunk, s = CHUNKS[c], state[c]
        after = [last]
        if step == "pick":
            blocks = [b for offset in chunk for b in arrived[offset]]
            last, *outgoing, s["meta"] = pick(chunk, after, place, blocks)
            s["pieces"] = across_x(outgoing, 1)
        elif step == "join":
            rows, width = s["pieces"][0].shape
            last, s["own"] = run(join_kernel, after, place, s["pieces"], [shaped(NX * rows, width)])
            s["other"] = swap(s["own"])
        elif step == "far":
            last, top, bottom = up_projection(2, 1, after, place, s["own"], s["other"], weights)
            s["far"] = shift(top, "y", NY, 1), shift(bottom, "y", NY, -1)
        elif step == "rest":
            last, s["minus"], s["mine"], s["plus"] = up_projection(
                3, 3, after, place, s["own"], s["other"], weights
            )
        elif step == "add":
            last, *near = run(
                add_kernel, after, place, [s["plus"], s["minus"], *s["far"]], [shaped(*s["plus"].shape)] * 2
            )
            s["near"] = shift(near[0], "y", NY, 1), shift(near[1], "y", NY, -1)
        elif step == "act":
            total, both = s["mine"].shape
            last, active = run(
                act_kernel, after, place, [s["mine"], *s["near"]], [shaped(total, both // 2)]
            )
            below, above = shift(active, "y", NY, 1), shift(active, "y", NY, -1)
            middle = total // 2
            s["active"] = [
                active,
                below,
                above,
                shift(below[:middle], "y", NY, 1),
                shift(above[middle:], "y", NY, -1),
            ]
        elif step == "down":
            last, *result = down_projection(
                after, place, s["active"], [swap(a) for a in s["active"]], w_down
            )
            s["back"] = across_x(result, -1)
        elif step == "mix":
            last, *partial = mix(chunk, after, place, s["meta"], s["back"])
            sums.update(zip(chunk, partial, strict=True))

    far = sums[NZ // 2]
    plus, minus = shift(far[:half], "z", NZ, 1), shift(far[half:], "z", NZ, -1)
    plus = jnp.concatenate([total_of(sums[3][:half], plus), sums[3][half:]])
    minus = jnp.concatenate([sums[-3][:half], total_of(sums[-3][half:], minus)])
    for step in (2, 1):
        plus = total_of(sums[step], shift(plus, "z", NZ, 1))
        minus = total_of(sums[-step], shift(minus, "z", NZ, -1))
    return total_of(sums[0], shift(plus, "z", NZ, 1), shift(minus, "z", NZ, -1))


def solution(mesh):
    split = Mesh(mesh.devices.reshape(NY, 2, NZ, NX), ("y", "core", "z", "x"))
    exp, ctx = ("z", "x"), ("y", "core")
    return jax.shard_map(
        per_device,
        mesh=split,
        in_specs=(
            P(exp, ctx),
            P(exp, None),
            P(exp, None),
            P(exp, ctx, None),
            P(exp, ctx, None),
            P(exp, None, ctx),
        ),
        out_specs=P(exp, ctx),
        check_vma=False,
    )
```

```python
import functools

import jax
import jax.numpy as jnp
from jax import lax
from jax.experimental import pallas as pl
from jax.experimental.pallas import tpu as pltpu
from jax.sharding import Mesh, PartitionSpec as P

BF16 = jnp.bfloat16
F32 = jnp.float32

NY, NZ, NX = 4, 8, 4
TOKENS = 256
TOP = 4
CAP = 41
META = 16
CHUNKS = ((0, -1, 1, -2, 2), (-3, 3, 4))
ORDER = (
    ("pick", 0),
    ("join", 0),
    ("pick", 1),
    ("far", 0),
    ("near", 0),
    ("join", 1),
    ("add", 0),
    ("far", 1),
    ("near", 1),
    ("mine", 0),
    ("mine", 1),
    ("add", 1),
    ("act", 0),
    ("act", 1),
    ("down", 1),
    ("down", 0),
    ("mix", 1),
    ("home", 0),
    ("mix", 0),
    ("home", 3),
    ("home", 2),
    ("home", 5),
    ("home", 4),
)
VMEM = 22 * 1024 * 1024
WORK = 20_000_000_000
WORKS = {("home", k): 1 for k in range(6)}
TOKEN = jax.ShapeDtypeStruct((8, 128), jnp.float32)


def rows_of(chunk):
    return -(-len(chunk) * CAP // 16) * 16


def lanes_of(chunk):
    return -(-rows_of(chunk) // 128) * 128


def shift(value, axis, size, step):
    return lax.ppermute(value, axis, [(i, (i + step) % size) for i in range(size)])


def swap(value):
    return lax.ppermute(value, "core", [(0, 1), (1, 0)])


def whole():
    return pl.BlockSpec(memory_space=pltpu.VMEM)


def shaped(*shape):
    return jax.ShapeDtypeStruct(shape, BF16)


def run(kernel, turn, place, operands, outs, scratch=(), grid=None, in_specs=None):
    work, after = turn
    in_specs = in_specs or [whole()] * len(operands)

    def body(place_ref, *refs):
        refs = refs[len(after) :]
        token_ref = refs[len(operands)]
        token_ref[...] = jnp.zeros_like(token_ref)
        kernel(place_ref, *refs[: len(operands)], *refs[len(operands) + 1 :])

    outs = [TOKEN] + list(outs)
    return pl.pallas_call(
        body,
        out_shape=outs,
        grid_spec=pltpu.PrefetchScalarGridSpec(
            num_scalar_prefetch=1,
            grid=grid or (1,),
            in_specs=[whole()] * len(after) + list(in_specs),
            out_specs=[pl.BlockSpec(o.shape, lambda *_, n=len(o.shape): (0,) * n) for o in outs],
            scratch_shapes=list(scratch),
        ),
        compiler_params=pltpu.CompilerParams(
            vmem_limit_bytes=VMEM, dimension_semantics=("arbitrary",) * len(grid or (1,))
        ),
        cost_estimate=pl.CostEstimate(flops=work, bytes_accessed=1, transcendentals=0),
    )(place, *after, *operands)


def pack_kernel(rows_ref, ids_ref, weight_ref, out_ref, ids, weight, sems):
    copies = [
        pltpu.make_async_copy(rows_ref, out_ref.at[pl.ds(0, TOKENS)], sems.at[0]),
        pltpu.make_async_copy(ids_ref, ids, sems.at[1]),
        pltpu.make_async_copy(weight_ref, weight, sems.at[2]),
    ]
    for copy in copies:
        copy.start()
    copies[1].wait()
    copies[2].wait()
    blank = jnp.zeros((META - 2 * TOP, TOKENS), F32)
    meta = jnp.concatenate([ids[...].astype(F32), weight[...], blank], axis=0)
    tail = jnp.zeros((META, out_ref.shape[1] - TOKENS), BF16)
    out_ref[TOKENS : TOKENS + META, :] = jnp.concatenate([meta.astype(BF16), tail], axis=1)
    copies[0].wait()


def pack(rows, ids, weight):
    return pl.pallas_call(
        pack_kernel,
        out_shape=shaped(TOKENS + META, rows.shape[1]),
        in_specs=[pl.BlockSpec(memory_space=pl.ANY)] * 3,
        out_specs=whole(),
        scratch_shapes=[
            pltpu.VMEM(ids.shape, ids.dtype),
            pltpu.VMEM(weight.shape, weight.dtype),
            pltpu.SemaphoreType.DMA((3,)),
        ],
        compiler_params=pltpu.CompilerParams(vmem_limit_bytes=VMEM),
    )(rows, ids, weight)


def halves_kernel(place_ref, gate_ref, up_ref, out_ref):
    half = gate_ref.shape[2]
    out_ref[:, 0:half] = gate_ref[0]
    out_ref[:, half : 2 * half] = up_ref[0]


def other_half(after, place, w_gate, w_up):
    _, width, hidden = w_gate.shape

    def block(k, place_ref):
        return (0, 0, 1 - place_ref[3])

    spec = pl.BlockSpec((1, width, hidden // 2), block)
    return run(
        halves_kernel, after, place, [w_gate, w_up], [shaped(width, hidden)], in_specs=[spec, spec]
    )


def places(meta, place_ref):
    ids = meta[0:TOP, :]
    weight = meta[TOP : 2 * TOP, :]
    hit, scale = [], []
    for j in range(NX):
        expert = place_ref[0] * NX + lax.rem(place_ref[1] + j, NX)
        same = (ids == expert.astype(F32)).astype(F32)
        hit.append(jnp.sum(same, axis=0, keepdims=True))
        scale.append(jnp.sum(same * weight, axis=0, keepdims=True))
    hit, scale = jnp.concatenate(hit, axis=0), jnp.concatenate(scale, axis=0)
    before = (
        lax.broadcasted_iota(jnp.int32, (TOKENS, TOKENS), 0)
        <= lax.broadcasted_iota(jnp.int32, (TOKENS, TOKENS), 1)
    ).astype(F32).astype(BF16)
    padded = jnp.concatenate([hit, jnp.zeros_like(hit)], axis=0).astype(BF16)
    rank = jnp.dot(padded, before, preferred_element_type=F32)[0:NX] - 1.0
    return hit, rank, scale


def pick_kernel(chunk, place_ref, *refs):
    rows = rows_of(chunk)
    blocks, out_refs, (meta_ref, picked, held) = refs[: -NX - 3], refs[-NX - 3 : -3], refs[-3:]
    taken = 0
    index = lax.broadcasted_iota(jnp.int32, (rows, TOKENS), 0).astype(F32)
    for i, offset in enumerate(chunk):
        if offset == NZ // 2:
            first, second = blocks[taken : taken + 2]
            taken += 2
            half = first.shape[0]
            held[i * TOKENS : i * TOKENS + half, :] = first[...]
            held[i * TOKENS + half : (i + 1) * TOKENS, :] = second[0 : TOKENS - half, :]
            meta = second[TOKENS - half : TOKENS - half + META, 0:TOKENS]
        else:
            block = blocks[taken]
            taken += 1
            held[i * TOKENS : (i + 1) * TOKENS, :] = block[0:TOKENS, :]
            meta = block[TOKENS : TOKENS + META, 0:TOKENS]
        meta_ref[i * META : (i + 1) * META, :] = meta
        hit, rank, _ = places(meta.astype(F32), place_ref)
        slot = jnp.where(hit > 0, rank + float(CAP * i), -1.0)
        for j in range(NX):
            picked[j * rows : (j + 1) * rows, i * TOKENS : (i + 1) * TOKENS] = (
                (index == slot[j : j + 1, :]).astype(F32).astype(BF16)
            )
    found = jnp.dot(picked[...], held[...], preferred_element_type=F32).astype(BF16)
    for j in range(NX):
        out_refs[j][...] = found[j * rows : (j + 1) * rows, :]


def pick(chunk, after, place, blocks):
    rows, count, width = rows_of(chunk), len(chunk), blocks[0].shape[1]
    return run(
        functools.partial(pick_kernel, chunk),
        after,
        place,
        blocks,
        [shaped(rows, width)] * NX + [shaped(count * META, TOKENS)],
        [pltpu.VMEM((NX * rows, count * TOKENS), BF16), pltpu.VMEM((count * TOKENS, width), BF16)],
    )


def mix_kernel(chunk, place_ref, meta_ref, *refs):
    rows, lanes = rows_of(chunk), lanes_of(chunk)
    returned, out_refs, (mixed, held) = refs[:NX], refs[NX:-2], refs[-2:]
    width = held.shape[1]
    for j in range(NX):
        held[j * lanes : j * lanes + rows, :] = returned[j][...]
        if lanes > rows:
            held[j * lanes + rows : (j + 1) * lanes, :] = jnp.zeros((lanes - rows, width), BF16)
    index = lax.broadcasted_iota(jnp.int32, (TOKENS, lanes), 1).astype(F32)
    for i in range(len(chunk)):
        meta = meta_ref[i * META : (i + 1) * META, :].astype(F32)
        hit, rank, scale = places(meta, place_ref)
        slot = jnp.where(hit > 0, rank + float(CAP * i), -1.0)
        both = jnp.concatenate([slot, scale], axis=0).T
        for j in range(NX):
            mixed[i * TOKENS : (i + 1) * TOKENS, j * lanes : (j + 1) * lanes] = jnp.where(
                index == both[:, j : j + 1], both[:, NX + j : NX + j + 1], 0.0
            ).astype(BF16)
    total = jnp.dot(mixed[...], held[...], preferred_element_type=F32).astype(BF16)
    half = TOKENS // 2
    for k, out_ref in enumerate(out_refs):
        out_ref[...] = total[k * half : (k + 1) * half, :]


def mix(chunk, after, place, meta, returned):
    lanes, count, width = lanes_of(chunk), len(chunk), returned[0].shape[1]
    return run(
        functools.partial(mix_kernel, chunk),
        after,
        place,
        [meta, *returned],
        [shaped(TOKENS // 2, width)] * (2 * count),
        [pltpu.VMEM((count * TOKENS, NX * lanes), BF16), pltpu.VMEM((NX * lanes, width), BF16)],
    )


def join_kernel(place_ref, *refs):
    rows = refs[0].shape[0]
    for j in range(NX):
        refs[NX][j * rows : (j + 1) * rows, :] = refs[j][...]


def up_kernel(place_ref, *refs):
    own, other, gate_ref, up_ref, gate2_ref, up2_ref = refs[:6]
    out_refs, held = refs[6:-1], refs[-1]
    width = own.shape[1]
    part = gate_ref.shape[2]

    @pl.when(pl.program_id(0) == 0)
    def _():
        held[:, 0:width] = own[...]
        held[:, width : 2 * width] = other[...]

    gate = jnp.dot(
        held[...], jnp.concatenate([gate_ref[0], gate2_ref[...]], axis=0), preferred_element_type=F32
    ).astype(BF16)
    up = jnp.dot(
        held[...], jnp.concatenate([up_ref[0], up2_ref[...]], axis=0), preferred_element_type=F32
    ).astype(BF16)
    if out_refs[0].shape[0] < held.shape[0]:
        half = out_refs[0].shape[0]
        for k in range(2):
            out_refs[k][:, 0:part] = gate[k * half : (k + 1) * half]
            out_refs[k][:, part : 2 * part] = up[k * half : (k + 1) * half]
    else:
        for k, out_ref in enumerate(out_refs):

            @pl.when(pl.program_id(0) == k)
            def _(out_ref=out_ref):
                out_ref[:, 0:part] = gate
                out_ref[:, part : 2 * part] = up


def up_projection(first, count, after, place, own, other, weights):
    w_gate, w_up, swapped = weights
    total, width = own.shape
    part = w_gate.shape[2] // (2 * NY)

    def column(k, place_ref):
        return lax.rem(place_ref[2] + first + 2 * k, NY)

    def own_block(k, place_ref):
        return (0, 0, place_ref[3] * NY + column(k, place_ref))

    def gate_block(k, place_ref):
        return (0, column(k, place_ref))

    def up_block(k, place_ref):
        return (0, NY + column(k, place_ref))

    outs = [shaped(total // 2, 2 * part)] * 2 if first == 2 else [shaped(total, 2 * part)] * count
    return run(
        up_kernel,
        after,
        place,
        [own, other, w_gate, w_up, swapped, swapped],
        outs,
        [pltpu.VMEM((total, 2 * width), BF16)],
        (count,),
        [whole()] * 2
        + [pl.BlockSpec((1, width, part), own_block)] * 2
        + [pl.BlockSpec((width, part), gate_block), pl.BlockSpec((width, part), up_block)],
    )


def add_kernel(place_ref, plus_ref, minus_ref, far_plus, far_minus, out_plus, out_minus):
    half = far_plus.shape[0]
    out_plus[0:half] = (plus_ref[0:half].astype(F32) + far_plus[...].astype(F32)).astype(BF16)
    out_plus[half:] = plus_ref[half:]
    out_minus[0:half] = minus_ref[0:half]
    out_minus[half:] = (minus_ref[half:].astype(F32) + far_minus[...].astype(F32)).astype(BF16)


def pair_kernel(place_ref, a, b, c, d, first_ref, second_ref):
    first_ref[...] = (a[...].astype(F32) + b[...].astype(F32)).astype(BF16)
    second_ref[...] = (c[...].astype(F32) + d[...].astype(F32)).astype(BF16)


def act_kernel(place_ref, own, plus, minus, out_ref):
    total = own[...].astype(F32) + plus[...].astype(F32) + minus[...].astype(F32)
    part = out_ref.shape[1]
    out_ref[...] = (jax.nn.silu(total[:, 0:part]) * total[:, part : 2 * part]).astype(BF16)


def down_kernel(count, place_ref, *refs):
    actives, weight_refs, out_refs, held = (
        refs[: 2 * count],
        refs[2 * count : 2 * count + 2 * NY],
        refs[2 * count + 2 * NY : -1],
        refs[-1],
    )
    part = weight_refs[0].shape[1]
    for c in range(2):
        for i in range(count):
            block = actives[c * count + i]
            if i < NY - 1:
                held[:, (c * NY + i) * part : (c * NY + i + 1) * part] = block[...]
            else:
                half = block.shape[0]
                start = (i - NY + 1) * half
                held[start : start + half, (c * NY + NY - 1) * part : (c * NY + NY) * part] = block[...]
    weight = jnp.concatenate([w[0] for w in weight_refs], axis=0)
    rows = out_refs[0].shape[0]
    result = jnp.dot(held[...], weight, preferred_element_type=F32).astype(BF16)
    for j in range(NX):
        out_refs[j][...] = result[j * rows : (j + 1) * rows, :]


def down_projection(after, place, own, other, w_down):
    total, part = own[0].shape
    width = w_down.shape[2]

    def weight_block(distance, flip):
        def at(k, place_ref):
            core = 1 - place_ref[3] if flip else place_ref[3]
            return (0, core * NY + lax.rem(place_ref[2] + distance, NY), 0)

        return pl.BlockSpec((1, part, width), at)

    actives = list(own) + list(other)
    return run(
        functools.partial(down_kernel, len(own)),
        after,
        place,
        actives + [w_down] * (2 * NY),
        [shaped(total // NX, width)] * NX,
        [pltpu.VMEM((total, 2 * NY * part), BF16)],
        None,
        [whole()] * len(actives)
        + [weight_block(d, flip) for flip in (False, True) for d in (0, NY - 1, 1, 2)],
    )


def total_of(*terms):
    return sum(t.astype(F32) for t in terms).astype(BF16)


def across_x(values, way):
    return [values[0]] + [shift(values[j], "x", NX, way * j) for j in range(1, NX)]


def per_device(moe_rows, expert_ids, route_weight, w_gate, w_up, w_down):
    place = jnp.stack([lax.axis_index(a) for a in ("z", "x", "y", "core")]).astype(jnp.int32)

    own = pack(moe_rows, expert_ids.T, route_weight.T)
    arrived = {0: (own,)}
    plus, minus = own, own
    for step in range(1, NZ // 2):
        plus, minus = shift(plus, "z", NZ, 1), shift(minus, "z", NZ, -1)
        arrived[-step], arrived[step] = (plus,), (minus,)
    last, swapped = other_half((WORK, []), place, w_gate, w_up)
    weights = (w_gate, w_up, swap(swapped))
    half = TOKENS // 2
    arrived[NZ // 2] = (
        shift(plus[:half], "z", NZ, 1),
        shift(minus[half:], "z", NZ, -1),
    )

    state = [{} for _ in CHUNKS]
    sums = {}
    for step, c in ORDER:
        chunk, s = (CHUNKS[c], state[c]) if step != "home" else (None, None)
        after = (WORKS.get((step, c), WORK), [last])
        if step == "pick":
            blocks = [b for offset in chunk for b in arrived[offset]]
            last, *outgoing, s["meta"] = pick(chunk, after, place, blocks)
            s["pieces"] = across_x(outgoing, 1)
        elif step == "join":
            rows, width = s["pieces"][0].shape
            last, s["own"] = run(join_kernel, after, place, s["pieces"], [shaped(NX * rows, width)])
            s["other"] = swap(s["own"])
        elif step == "far":
            last, top, bottom = up_projection(2, 1, after, place, s["own"], s["other"], weights)
            s["far"] = shift(top, "y", NY, 1), shift(bottom, "y", NY, -1)
        elif step == "near":
            last, s["minus"], s["plus"] = up_projection(3, 2, after, place, s["own"], s["other"], weights)
        elif step == "mine":
            last, s["mine"] = up_projection(0, 1, after, place, s["own"], s["other"], weights)
        elif step == "add":
            last, *near = run(
                add_kernel, after, place, [s["plus"], s["minus"], *s["far"]], [shaped(*s["plus"].shape)] * 2
            )
            s["near"] = shift(near[0], "y", NY, 1), shift(near[1], "y", NY, -1)
        elif step == "act":
            total, both = s["mine"].shape
            last, active = run(
                act_kernel, after, place, [s["mine"], *s["near"]], [shaped(total, both // 2)]
            )
            below, above = shift(active, "y", NY, 1), shift(active, "y", NY, -1)
            middle = total // 2
            s["active"] = [
                active,
                below,
                above,
                shift(below[:middle], "y", NY, 1),
                shift(above[middle:], "y", NY, -1),
            ]
        elif step == "down":
            last, *result = down_projection(
                after, place, s["active"], [swap(a) for a in s["active"]], w_down
            )
            s["back"] = across_x(result, -1)
        elif step == "mix":
            last, *partial = mix(chunk, after, place, s["meta"], s["back"])
            sums.update(zip(chunk, zip(partial[0::2], partial[1::2]), strict=True))
        elif step == "home":
            h, d = c % 2, 3 - c // 2
            if d == 3 and h == 0:
                moving = [
                    [shift(sums[4][0], "z", NZ, 1), shift(sums[4][1], "z", NZ, -1)],
                    [shift(sums[3][1], "z", NZ, 1), shift(sums[-3][0], "z", NZ, -1)],
                ]
            if d < 3 or h == 0:
                terms = [sums[d][h], moving[h][0], sums[-d][1 - h], moving[h][1]]
                last, up, down = run(pair_kernel, after, place, terms, [shaped(*t.shape) for t in terms[::2]])
                moving[h] = [shift(up, "z", NZ, 1), shift(down, "z", NZ, -1)]

    return jnp.concatenate([total_of(sums[0][h], moving[h][0], moving[1 - h][1]) for h in range(2)])


def solution(mesh):
    split = Mesh(mesh.devices.reshape(NY, 2, NZ, NX), ("y", "core", "z", "x"))
    exp, ctx = ("z", "x"), ("y", "core")
    return jax.shard_map(
        per_device,
        mesh=split,
        in_specs=(
            P(exp, ctx),
            P(exp, None),
            P(exp, None),
            P(exp, ctx, None),
            P(exp, ctx, None),
            P(exp, None, ctx),
        ),
        out_specs=P(exp, ctx),
        check_vma=False,
    )
```

```python
import functools

import jax
import jax.numpy as jnp
from jax import lax
from jax.experimental import pallas as pl
from jax.experimental.pallas import tpu as pltpu
from jax.sharding import Mesh, PartitionSpec as P

BF16 = jnp.bfloat16
F32 = jnp.float32

NY, NZ, NX = 4, 8, 4
TOKENS = 256
TOP = 4
CAP = 41
META = 16
CHUNKS = ((0, -1, 1, -2, 2), (-3, 3, 4))
ORDER = (
    ("pick", 0),
    ("join", 0),
    ("pick", 1),
    ("far", 0),
    ("near", 0),
    ("join", 1),
    ("add", 0),
    ("far", 1),
    ("near", 1),
    ("mine", 0),
    ("mine", 1),
    ("add", 1),
    ("act", 0),
    ("act", 1),
    ("down", 1),
    ("down", 0),
    ("mix", 1),
    ("home", 0),
    ("mix", 0),
    ("home", 3),
    ("home", 2),
    ("rest", 0),
    ("home", 5),
    ("home", 4),
)
VMEM = 22 * 1024 * 1024
WORK = 20_000_000_000
WORKS = {("home", k): 1 for k in range(6)}
TOKEN = jax.ShapeDtypeStruct((8, 128), jnp.float32)


def rows_of(chunk):
    return -(-len(chunk) * CAP // 16) * 16


def lanes_of(chunk):
    return -(-rows_of(chunk) // 128) * 128


def shift(value, axis, size, step):
    return lax.ppermute(value, axis, [(i, (i + step) % size) for i in range(size)])


def swap(value):
    return lax.ppermute(value, "core", [(0, 1), (1, 0)])


def whole():
    return pl.BlockSpec(memory_space=pltpu.VMEM)


def shaped(*shape):
    return jax.ShapeDtypeStruct(shape, BF16)


def run(kernel, turn, place, operands, outs, scratch=(), grid=None, in_specs=None):
    work, after = turn
    in_specs = in_specs or [whole()] * len(operands)

    def body(place_ref, *refs):
        refs = refs[len(after) :]
        token_ref = refs[len(operands)]
        token_ref[...] = jnp.zeros_like(token_ref)
        kernel(place_ref, *refs[: len(operands)], *refs[len(operands) + 1 :])

    outs = [TOKEN] + list(outs)
    return pl.pallas_call(
        body,
        out_shape=outs,
        grid_spec=pltpu.PrefetchScalarGridSpec(
            num_scalar_prefetch=1,
            grid=grid or (1,),
            in_specs=[whole()] * len(after) + list(in_specs),
            out_specs=[pl.BlockSpec(o.shape, lambda *_, n=len(o.shape): (0,) * n) for o in outs],
            scratch_shapes=list(scratch),
        ),
        compiler_params=pltpu.CompilerParams(
            vmem_limit_bytes=VMEM, dimension_semantics=("arbitrary",) * len(grid or (1,))
        ),
        cost_estimate=pl.CostEstimate(flops=work, bytes_accessed=1, transcendentals=0),
    )(place, *after, *operands)


def pack_kernel(rows_ref, ids_ref, weight_ref, out_ref, ids, weight, sems):
    copies = [
        pltpu.make_async_copy(rows_ref, out_ref.at[pl.ds(0, TOKENS)], sems.at[0]),
        pltpu.make_async_copy(ids_ref, ids, sems.at[1]),
        pltpu.make_async_copy(weight_ref, weight, sems.at[2]),
    ]
    for copy in copies:
        copy.start()
    copies[1].wait()
    copies[2].wait()
    blank = jnp.zeros((META - 2 * TOP, TOKENS), F32)
    meta = jnp.concatenate([ids[...].astype(F32), weight[...], blank], axis=0)
    tail = jnp.zeros((META, out_ref.shape[1] - TOKENS), BF16)
    out_ref[TOKENS : TOKENS + META, :] = jnp.concatenate([meta.astype(BF16), tail], axis=1)
    copies[0].wait()


def pack(rows, ids, weight):
    return pl.pallas_call(
        pack_kernel,
        out_shape=shaped(TOKENS + META, rows.shape[1]),
        in_specs=[pl.BlockSpec(memory_space=pl.ANY)] * 3,
        out_specs=whole(),
        scratch_shapes=[
            pltpu.VMEM(ids.shape, ids.dtype),
            pltpu.VMEM(weight.shape, weight.dtype),
            pltpu.SemaphoreType.DMA((3,)),
        ],
        compiler_params=pltpu.CompilerParams(vmem_limit_bytes=60 * 1024 * 1024),
    )(rows, ids, weight)


def halves_kernel(place_ref, gate_ref, up_ref, out_ref):
    half = gate_ref.shape[2]
    out_ref[:, 0:half] = gate_ref[0]
    out_ref[:, half : 2 * half] = up_ref[0]


def other_half(after, place, w_gate, w_up):
    _, width, hidden = w_gate.shape

    def block(k, place_ref):
        return (0, 0, 1 - place_ref[3])

    spec = pl.BlockSpec((1, width, hidden // 2), block)
    return run(
        halves_kernel, after, place, [w_gate, w_up], [shaped(width, hidden)], in_specs=[spec, spec]
    )


def places(meta, place_ref):
    ids = meta[0:TOP, :]
    weight = meta[TOP : 2 * TOP, :]
    hit, scale = [], []
    for j in range(NX):
        expert = place_ref[0] * NX + lax.rem(place_ref[1] + j, NX)
        same = (ids == expert.astype(F32)).astype(F32)
        hit.append(jnp.sum(same, axis=0, keepdims=True))
        scale.append(jnp.sum(same * weight, axis=0, keepdims=True))
    hit, scale = jnp.concatenate(hit, axis=0), jnp.concatenate(scale, axis=0)
    before = (
        lax.broadcasted_iota(jnp.int32, (TOKENS, TOKENS), 0)
        <= lax.broadcasted_iota(jnp.int32, (TOKENS, TOKENS), 1)
    ).astype(F32).astype(BF16)
    padded = jnp.concatenate([hit, jnp.zeros_like(hit)], axis=0).astype(BF16)
    rank = jnp.dot(padded, before, preferred_element_type=F32)[0:NX] - 1.0
    return hit, rank, scale


def pick_kernel(chunk, place_ref, *refs):
    rows = rows_of(chunk)
    blocks, out_refs, (meta_ref, picked, held) = refs[: -NX - 3], refs[-NX - 3 : -3], refs[-3:]
    taken = 0
    index = lax.broadcasted_iota(jnp.int32, (rows, TOKENS), 0).astype(F32)
    for i, offset in enumerate(chunk):
        if offset == NZ // 2:
            first, second = blocks[taken : taken + 2]
            taken += 2
            half = first.shape[0]
            held[i * TOKENS : i * TOKENS + half, :] = first[...]
            held[i * TOKENS + half : (i + 1) * TOKENS, :] = second[0 : TOKENS - half, :]
            meta = second[TOKENS - half : TOKENS - half + META, 0:TOKENS]
        else:
            block = blocks[taken]
            taken += 1
            held[i * TOKENS : (i + 1) * TOKENS, :] = block[0:TOKENS, :]
            meta = block[TOKENS : TOKENS + META, 0:TOKENS]
        meta_ref[i * META : (i + 1) * META, :] = meta
        hit, rank, _ = places(meta.astype(F32), place_ref)
        slot = jnp.where(hit > 0, rank + float(CAP * i), -1.0)
        for j in range(NX):
            picked[j * rows : (j + 1) * rows, i * TOKENS : (i + 1) * TOKENS] = (
                (index == slot[j : j + 1, :]).astype(F32).astype(BF16)
            )
    found = jnp.dot(picked[...], held[...], preferred_element_type=F32).astype(BF16)
    for j in range(NX):
        out_refs[j][...] = found[j * rows : (j + 1) * rows, :]


def pick(chunk, after, place, blocks):
    rows, count, width = rows_of(chunk), len(chunk), blocks[0].shape[1]
    return run(
        functools.partial(pick_kernel, chunk),
        after,
        place,
        blocks,
        [shaped(rows, width)] * NX + [shaped(count * META, TOKENS)],
        [pltpu.VMEM((NX * rows, count * TOKENS), BF16), pltpu.VMEM((count * TOKENS, width), BF16)],
    )


def mix_kernel(chunk, part, place_ref, meta_ref, *refs):
    rows, lanes = rows_of(chunk), lanes_of(chunk)
    returned, out_refs, (mixed, held) = refs[:NX], refs[NX:-2], refs[-2:]
    width = held.shape[1]
    for j in range(NX):
        held[j * lanes : j * lanes + rows, :] = returned[j][...]
        if lanes > rows:
            held[j * lanes + rows : (j + 1) * lanes, :] = jnp.zeros((lanes - rows, width), BF16)
    index = lax.broadcasted_iota(jnp.int32, (TOKENS, lanes), 1).astype(F32)
    for n, i in enumerate(part):
        meta = meta_ref[i * META : (i + 1) * META, :].astype(F32)
        hit, rank, scale = places(meta, place_ref)
        slot = jnp.where(hit > 0, rank + float(CAP * i), -1.0)
        both = jnp.concatenate([slot, scale], axis=0).T
        for j in range(NX):
            mixed[n * TOKENS : (n + 1) * TOKENS, j * lanes : (j + 1) * lanes] = jnp.where(
                index == both[:, j : j + 1], both[:, NX + j : NX + j + 1], 0.0
            ).astype(BF16)
    total = jnp.dot(mixed[...], held[...], preferred_element_type=F32).astype(BF16)
    half = TOKENS // 2
    for k, out_ref in enumerate(out_refs):
        out_ref[...] = total[k * half : (k + 1) * half, :]


def mix(chunk, part, after, place, meta, returned):
    lanes, count, width = lanes_of(chunk), len(part), returned[0].shape[1]
    return run(
        functools.partial(mix_kernel, chunk, part),
        after,
        place,
        [meta, *returned],
        [shaped(TOKENS // 2, width)] * (2 * count),
        [pltpu.VMEM((count * TOKENS, NX * lanes), BF16), pltpu.VMEM((NX * lanes, width), BF16)],
    )


def join_kernel(place_ref, *refs):
    rows = refs[0].shape[0]
    for j in range(NX):
        refs[NX][j * rows : (j + 1) * rows, :] = refs[j][...]


def up_kernel(place_ref, *refs):
    own, other, gate_ref, up_ref, gate2_ref, up2_ref = refs[:6]
    out_refs, held = refs[6:-1], refs[-1]
    width = own.shape[1]
    part = gate_ref.shape[2]

    @pl.when(pl.program_id(0) == 0)
    def _():
        held[:, 0:width] = own[...]
        held[:, width : 2 * width] = other[...]

    gate = jnp.dot(
        held[...], jnp.concatenate([gate_ref[0], gate2_ref[...]], axis=0), preferred_element_type=F32
    ).astype(BF16)
    up = jnp.dot(
        held[...], jnp.concatenate([up_ref[0], up2_ref[...]], axis=0), preferred_element_type=F32
    ).astype(BF16)
    if out_refs[0].shape[0] < held.shape[0]:
        half = out_refs[0].shape[0]
        for k in range(2):
            out_refs[k][:, 0:part] = gate[k * half : (k + 1) * half]
            out_refs[k][:, part : 2 * part] = up[k * half : (k + 1) * half]
    else:
        for k, out_ref in enumerate(out_refs):

            @pl.when(pl.program_id(0) == k)
            def _(out_ref=out_ref):
                out_ref[:, 0:part] = gate
                out_ref[:, part : 2 * part] = up


def up_projection(first, count, after, place, own, other, weights):
    w_gate, w_up, swapped = weights
    total, width = own.shape
    part = w_gate.shape[2] // (2 * NY)

    def column(k, place_ref):
        return lax.rem(place_ref[2] + first + 2 * k, NY)

    def own_block(k, place_ref):
        return (0, 0, place_ref[3] * NY + column(k, place_ref))

    def gate_block(k, place_ref):
        return (0, column(k, place_ref))

    def up_block(k, place_ref):
        return (0, NY + column(k, place_ref))

    outs = [shaped(total // 2, 2 * part)] * 2 if first == 2 else [shaped(total, 2 * part)] * count
    return run(
        up_kernel,
        after,
        place,
        [own, other, w_gate, w_up, swapped, swapped],
        outs,
        [pltpu.VMEM((total, 2 * width), BF16)],
        (count,),
        [whole()] * 2
        + [pl.BlockSpec((1, width, part), own_block)] * 2
        + [pl.BlockSpec((width, part), gate_block), pl.BlockSpec((width, part), up_block)],
    )


def add_kernel(place_ref, plus_ref, minus_ref, far_plus, far_minus, out_plus, out_minus):
    half = far_plus.shape[0]
    out_plus[0:half] = (plus_ref[0:half].astype(F32) + far_plus[...].astype(F32)).astype(BF16)
    out_plus[half:] = plus_ref[half:]
    out_minus[0:half] = minus_ref[0:half]
    out_minus[half:] = (minus_ref[half:].astype(F32) + far_minus[...].astype(F32)).astype(BF16)


def pair_kernel(place_ref, a, b, c, d, first_ref, second_ref):
    first_ref[...] = (a[...].astype(F32) + b[...].astype(F32)).astype(BF16)
    second_ref[...] = (c[...].astype(F32) + d[...].astype(F32)).astype(BF16)


def act_kernel(place_ref, own, plus, minus, out_ref):
    total = own[...].astype(F32) + plus[...].astype(F32) + minus[...].astype(F32)
    part = out_ref.shape[1]
    out_ref[...] = (jax.nn.silu(total[:, 0:part]) * total[:, part : 2 * part]).astype(BF16)


def down_kernel(count, place_ref, *refs):
    actives, weight_refs, out_refs, held = (
        refs[: 2 * count],
        refs[2 * count : 2 * count + 2 * NY],
        refs[2 * count + 2 * NY : -1],
        refs[-1],
    )
    part = weight_refs[0].shape[1]
    for c in range(2):
        for i in range(count):
            block = actives[c * count + i]
            if i < NY - 1:
                held[:, (c * NY + i) * part : (c * NY + i + 1) * part] = block[...]
            else:
                half = block.shape[0]
                start = (i - NY + 1) * half
                held[start : start + half, (c * NY + NY - 1) * part : (c * NY + NY) * part] = block[...]
    weight = jnp.concatenate([w[0] for w in weight_refs], axis=0)
    rows = out_refs[0].shape[0]
    result = jnp.dot(held[...], weight, preferred_element_type=F32).astype(BF16)
    for j in range(NX):
        out_refs[j][...] = result[j * rows : (j + 1) * rows, :]


def down_projection(after, place, own, other, w_down):
    total, part = own[0].shape
    width = w_down.shape[2]

    def weight_block(distance, flip):
        def at(k, place_ref):
            core = 1 - place_ref[3] if flip else place_ref[3]
            return (0, core * NY + lax.rem(place_ref[2] + distance, NY), 0)

        return pl.BlockSpec((1, part, width), at)

    actives = list(own) + list(other)
    return run(
        functools.partial(down_kernel, len(own)),
        after,
        place,
        actives + [w_down] * (2 * NY),
        [shaped(total // NX, width)] * NX,
        [pltpu.VMEM((total, 2 * NY * part), BF16)],
        None,
        [whole()] * len(actives)
        + [weight_block(d, flip) for flip in (False, True) for d in (0, NY - 1, 1, 2)],
    )


def total_of(*terms):
    return sum(t.astype(F32) for t in terms).astype(BF16)


def across_x(values, way):
    return [values[0]] + [shift(values[j], "x", NX, way * j) for j in range(1, NX)]


def per_device(moe_rows, expert_ids, route_weight, w_gate, w_up, w_down):
    place = jnp.stack([lax.axis_index(a) for a in ("z", "x", "y", "core")]).astype(jnp.int32)

    own = pack(moe_rows, expert_ids.T, route_weight.T)
    arrived = {0: (own,)}
    plus, minus = own, own
    for step in range(1, NZ // 2):
        plus, minus = shift(plus, "z", NZ, 1), shift(minus, "z", NZ, -1)
        arrived[-step], arrived[step] = (plus,), (minus,)
    last, swapped = other_half((WORK, []), place, w_gate, w_up)
    weights = (w_gate, w_up, swap(swapped))
    half = TOKENS // 2
    arrived[NZ // 2] = (
        shift(plus[:half], "z", NZ, 1),
        shift(minus[half:], "z", NZ, -1),
    )

    state = [{} for _ in CHUNKS]
    sums = {}
    for step, c in ORDER:
        chunk, s = (CHUNKS[c], state[c]) if step != "home" else (None, None)
        after = (WORKS.get((step, c), WORK), [last])
        if step == "pick":
            blocks = [b for offset in chunk for b in arrived[offset]]
            last, *outgoing, s["meta"] = pick(chunk, after, place, blocks)
            s["pieces"] = across_x(outgoing, 1)
        elif step == "join":
            rows, width = s["pieces"][0].shape
            last, s["own"] = run(join_kernel, after, place, s["pieces"], [shaped(NX * rows, width)])
            s["other"] = swap(s["own"])
        elif step == "far":
            last, top, bottom = up_projection(2, 1, after, place, s["own"], s["other"], weights)
            s["far"] = shift(top, "y", NY, 1), shift(bottom, "y", NY, -1)
        elif step == "near":
            last, s["minus"], s["plus"] = up_projection(3, 2, after, place, s["own"], s["other"], weights)
        elif step == "mine":
            last, s["mine"] = up_projection(0, 1, after, place, s["own"], s["other"], weights)
        elif step == "add":
            last, *near = run(
                add_kernel, after, place, [s["plus"], s["minus"], *s["far"]], [shaped(*s["plus"].shape)] * 2
            )
            s["near"] = shift(near[0], "y", NY, 1), shift(near[1], "y", NY, -1)
        elif step == "act":
            total, both = s["mine"].shape
            last, active = run(
                act_kernel, after, place, [s["mine"], *s["near"]], [shaped(total, both // 2)]
            )
            below, above = shift(active, "y", NY, 1), shift(active, "y", NY, -1)
            middle = total // 2
            s["active"] = [
                active,
                below,
                above,
                shift(below[:middle], "y", NY, 1),
                shift(above[middle:], "y", NY, -1),
            ]
        elif step == "down":
            last, *result = down_projection(
                after, place, s["active"], [swap(a) for a in s["active"]], w_down
            )
            s["back"] = across_x(result, -1)
        elif step in ("mix", "rest"):
            cut = 0 if c else 3
            part = range(cut, len(chunk)) if step == "mix" else range(cut)
            last, *partial = mix(chunk, part, after, place, s["meta"], s["back"])
            sums.update((chunk[i], partial[2 * n : 2 * n + 2]) for n, i in enumerate(part))
        elif step == "home":
            h, d = c % 2, 3 - c // 2
            if d == 3 and h == 0:
                moving = [
                    [shift(sums[4][0], "z", NZ, 1), shift(sums[4][1], "z", NZ, -1)],
                    [shift(sums[3][1], "z", NZ, 1), shift(sums[-3][0], "z", NZ, -1)],
                ]
            if d < 3 or h == 0:
                terms = [sums[d][h], moving[h][0], sums[-d][1 - h], moving[h][1]]
                last, up, down = run(pair_kernel, after, place, terms, [shaped(*t.shape) for t in terms[::2]])
                moving[h] = [shift(up, "z", NZ, 1), shift(down, "z", NZ, -1)]

    return jnp.concatenate([total_of(sums[0][h], moving[h][0], moving[1 - h][1]) for h in range(2)])


def solution(mesh):
    split = Mesh(mesh.devices.reshape(NY, 2, NZ, NX), ("y", "core", "z", "x"))
    exp, ctx = ("z", "x"), ("y", "core")
    return jax.shard_map(
        per_device,
        mesh=split,
        in_specs=(
            P(exp, ctx),
            P(exp, None),
            P(exp, None),
            P(exp, ctx, None),
            P(exp, ctx, None),
            P(exp, None, ctx),
        ),
        out_specs=P(exp, ctx),
        check_vma=False,
    )
```

```python
import functools

import jax
import jax.numpy as jnp
from jax import lax
from jax.experimental import pallas as pl
from jax.experimental.pallas import tpu as pltpu
from jax.sharding import Mesh, PartitionSpec as P

BF16 = jnp.bfloat16
F32 = jnp.float32

NY, NZ, NX = 4, 8, 4
TOKENS = 256
TOP = 4
CAP = 41
META = 16
CHUNKS = ((-2, 2, 0, -1, 1), (-3, 3, 4))
PARTS = ((96, 112), (128,))
ORDER = (
    ("pick", 0),
    ("join", 0),
    ("pick", 1),
    ("far", 0),
    ("near", 0),
    ("join", 1),
    ("add", 0),
    ("far", 1),
    ("near", 1),
    ("mine", 0),
    ("mine", 1),
    ("add", 1),
    ("act", 0),
    ("act", 1),
    ("down", 1),
    ("down", 0),
    ("mix", 1),
    ("mix", 0),
    ("home", 0),
    ("home", 3),
    ("home", 2),
    ("rest", 0),
    ("home", 5),
    ("home", 4),
)
VMEM = 22 * 1024 * 1024
WORK = 20_000_000_000
WORKS = {("home", k): 1 for k in range(6)}
TOKEN = jax.ShapeDtypeStruct((8, 128), jnp.float32)


def rows_of(chunk):
    return -(-len(chunk) * CAP // 16) * 16


def shift(value, axis, size, step):
    return lax.ppermute(value, axis, [(i, (i + step) % size) for i in range(size)])


def swap(value):
    return lax.ppermute(value, "core", [(0, 1), (1, 0)])


def whole():
    return pl.BlockSpec(memory_space=pltpu.VMEM)


def shaped(*shape):
    return jax.ShapeDtypeStruct(shape, BF16)


def run(kernel, turn, place, operands, outs, scratch=(), grid=None, in_specs=None):
    work, after = turn
    in_specs = in_specs or [whole()] * len(operands)

    def body(place_ref, *refs):
        refs = refs[len(after) :]
        token_ref = refs[len(operands)]
        token_ref[...] = jnp.zeros_like(token_ref)
        kernel(place_ref, *refs[: len(operands)], *refs[len(operands) + 1 :])

    outs = [TOKEN] + list(outs)
    return pl.pallas_call(
        body,
        out_shape=outs,
        grid_spec=pltpu.PrefetchScalarGridSpec(
            num_scalar_prefetch=1,
            grid=grid or (1,),
            in_specs=[whole()] * len(after) + list(in_specs),
            out_specs=[pl.BlockSpec(o.shape, lambda *_, n=len(o.shape): (0,) * n) for o in outs],
            scratch_shapes=list(scratch),
        ),
        compiler_params=pltpu.CompilerParams(
            vmem_limit_bytes=VMEM, dimension_semantics=("arbitrary",) * len(grid or (1,))
        ),
        cost_estimate=pl.CostEstimate(flops=work, bytes_accessed=1, transcendentals=0),
    )(place, *after, *operands)


def pack_kernel(rows_ref, ids_ref, weight_ref, out_ref, ids, weight, sems):
    copies = [
        pltpu.make_async_copy(rows_ref, out_ref.at[pl.ds(0, TOKENS)], sems.at[0]),
        pltpu.make_async_copy(ids_ref, ids, sems.at[1]),
        pltpu.make_async_copy(weight_ref, weight, sems.at[2]),
    ]
    for copy in copies:
        copy.start()
    copies[1].wait()
    copies[2].wait()
    blank = jnp.zeros((META - 2 * TOP, TOKENS), F32)
    meta = jnp.concatenate([ids[...].astype(F32), weight[...], blank], axis=0)
    tail = jnp.zeros((META, out_ref.shape[1] - TOKENS), BF16)
    out_ref[TOKENS : TOKENS + META, :] = jnp.concatenate([meta.astype(BF16), tail], axis=1)
    copies[0].wait()


def pack(rows, ids, weight):
    return pl.pallas_call(
        pack_kernel,
        out_shape=shaped(TOKENS + META, rows.shape[1]),
        in_specs=[pl.BlockSpec(memory_space=pl.ANY)] * 3,
        out_specs=whole(),
        scratch_shapes=[
            pltpu.VMEM(ids.shape, ids.dtype),
            pltpu.VMEM(weight.shape, weight.dtype),
            pltpu.SemaphoreType.DMA((3,)),
        ],
        compiler_params=pltpu.CompilerParams(vmem_limit_bytes=60 * 1024 * 1024),
    )(rows, ids, weight)


def halves_kernel(place_ref, gate_ref, up_ref, out_ref):
    half = gate_ref.shape[2]
    out_ref[:, 0:half] = gate_ref[0]
    out_ref[:, half : 2 * half] = up_ref[0]


def other_half(after, place, w_gate, w_up):
    _, width, hidden = w_gate.shape

    def block(k, place_ref):
        return (0, 0, 1 - place_ref[3])

    spec = pl.BlockSpec((1, width, hidden // 2), block)
    return run(
        halves_kernel, after, place, [w_gate, w_up], [shaped(width, hidden)], in_specs=[spec, spec]
    )


def places(meta, place_ref):
    ids = meta[0:TOP, :]
    weight = meta[TOP : 2 * TOP, :]
    hit, scale = [], []
    for j in range(NX):
        expert = place_ref[0] * NX + lax.rem(place_ref[1] + j, NX)
        same = (ids == expert.astype(F32)).astype(F32)
        hit.append(jnp.sum(same, axis=0, keepdims=True))
        scale.append(jnp.sum(same * weight, axis=0, keepdims=True))
    hit, scale = jnp.concatenate(hit, axis=0), jnp.concatenate(scale, axis=0)
    before = (
        lax.broadcasted_iota(jnp.int32, (TOKENS, TOKENS), 0)
        <= lax.broadcasted_iota(jnp.int32, (TOKENS, TOKENS), 1)
    ).astype(F32).astype(BF16)
    padded = jnp.concatenate([hit, jnp.zeros_like(hit)], axis=0).astype(BF16)
    rank = jnp.dot(padded, before, preferred_element_type=F32)[0:NX] - 1.0
    return hit, rank, scale


def pick_kernel(chunk, place_ref, *refs):
    rows = rows_of(chunk)
    blocks, out_refs, (meta_ref, picked, held) = refs[: -NX - 3], refs[-NX - 3 : -3], refs[-3:]
    taken = 0
    index = lax.broadcasted_iota(jnp.int32, (rows, TOKENS), 0).astype(F32)
    for i, offset in enumerate(chunk):
        if offset == NZ // 2:
            first, second = blocks[taken : taken + 2]
            taken += 2
            half = first.shape[0]
            held[i * TOKENS : i * TOKENS + half, :] = first[...]
            held[i * TOKENS + half : (i + 1) * TOKENS, :] = second[0 : TOKENS - half, :]
            meta = second[TOKENS - half : TOKENS - half + META, 0:TOKENS]
        else:
            block = blocks[taken]
            taken += 1
            held[i * TOKENS : (i + 1) * TOKENS, :] = block[0:TOKENS, :]
            meta = block[TOKENS : TOKENS + META, 0:TOKENS]
        meta_ref[i * META : (i + 1) * META, :] = meta
        hit, rank, _ = places(meta.astype(F32), place_ref)
        slot = jnp.where(hit > 0, rank + float(CAP * i), -1.0)
        for j in range(NX):
            picked[j * rows : (j + 1) * rows, i * TOKENS : (i + 1) * TOKENS] = (
                (index == slot[j : j + 1, :]).astype(F32).astype(BF16)
            )
    found = jnp.dot(picked[...], held[...], preferred_element_type=F32).astype(BF16)
    for j in range(NX):
        out_refs[j][...] = found[j * rows : (j + 1) * rows, :]


def pick(chunk, after, place, blocks):
    rows, count, width = rows_of(chunk), len(chunk), blocks[0].shape[1]
    return run(
        functools.partial(pick_kernel, chunk),
        after,
        place,
        blocks,
        [shaped(rows, width)] * NX + [shaped(count * META, TOKENS)],
        [pltpu.VMEM((NX * rows, count * TOKENS), BF16), pltpu.VMEM((count * TOKENS, width), BF16)],
    )


def mix_kernel(chunk, part, place_ref, meta_ref, *refs):
    pieces, out_refs, (mixed, held) = refs[: -2 * len(part) - 2], refs[-2 * len(part) - 2 : -2], refs[-2:]
    lanes, width = held.shape[0] // NX, held.shape[1]
    for j in range(NX):
        start = j * lanes
        for piece in pieces[j::NX]:
            rows = piece.shape[0]
            held[start : start + rows, :] = piece[...]
            start += rows
        if start < (j + 1) * lanes:
            held[start : (j + 1) * lanes, :] = jnp.zeros(((j + 1) * lanes - start, width), BF16)
    index = lax.broadcasted_iota(jnp.int32, (TOKENS, lanes), 1).astype(F32)
    for n, i in enumerate(part):
        meta = meta_ref[i * META : (i + 1) * META, :].astype(F32)
        hit, rank, scale = places(meta, place_ref)
        slot = jnp.where(hit > 0, rank + float(CAP * i), -1.0)
        both = jnp.concatenate([slot, scale], axis=0).T
        for j in range(NX):
            mixed[n * TOKENS : (n + 1) * TOKENS, j * lanes : (j + 1) * lanes] = jnp.where(
                index == both[:, j : j + 1], both[:, NX + j : NX + j + 1], 0.0
            ).astype(BF16)
    total = jnp.dot(mixed[...], held[...], preferred_element_type=F32).astype(BF16)
    half = TOKENS // 2
    for k, out_ref in enumerate(out_refs):
        out_ref[...] = total[k * half : (k + 1) * half, :]


def mix(chunk, part, after, place, meta, returned):
    rows, count, width = sum(piece[0].shape[0] for piece in returned), len(part), returned[0][0].shape[1]
    lanes = -(-rows // 128) * 128
    return run(
        functools.partial(mix_kernel, chunk, part),
        after,
        place,
        [meta, *sum(returned, [])],
        [shaped(TOKENS // 2, width)] * (2 * count),
        [pltpu.VMEM((count * TOKENS, NX * lanes), BF16), pltpu.VMEM((NX * lanes, width), BF16)],
    )


def join_kernel(place_ref, *refs):
    rows = refs[0].shape[0]
    for j in range(NX):
        refs[NX][j * rows : (j + 1) * rows, :] = refs[j][...]


def up_kernel(place_ref, *refs):
    own, other, gate_ref, up_ref, gate2_ref, up2_ref = refs[:6]
    out_refs, held = refs[6:-1], refs[-1]
    width = own.shape[1]
    part = gate_ref.shape[2]

    @pl.when(pl.program_id(0) == 0)
    def _():
        held[:, 0:width] = own[...]
        held[:, width : 2 * width] = other[...]

    gate = jnp.dot(
        held[...], jnp.concatenate([gate_ref[0], gate2_ref[...]], axis=0), preferred_element_type=F32
    ).astype(BF16)
    up = jnp.dot(
        held[...], jnp.concatenate([up_ref[0], up2_ref[...]], axis=0), preferred_element_type=F32
    ).astype(BF16)
    if out_refs[0].shape[0] < held.shape[0]:
        half = out_refs[0].shape[0]
        for k in range(2):
            out_refs[k][:, 0:part] = gate[k * half : (k + 1) * half]
            out_refs[k][:, part : 2 * part] = up[k * half : (k + 1) * half]
    else:
        for k, out_ref in enumerate(out_refs):

            @pl.when(pl.program_id(0) == k)
            def _(out_ref=out_ref):
                out_ref[:, 0:part] = gate
                out_ref[:, part : 2 * part] = up


def up_projection(first, count, after, place, own, other, weights):
    w_gate, w_up, swapped = weights
    total, width = own.shape
    part = w_gate.shape[2] // (2 * NY)

    def column(k, place_ref):
        return lax.rem(place_ref[2] + first + 2 * k, NY)

    def own_block(k, place_ref):
        return (0, 0, place_ref[3] * NY + column(k, place_ref))

    def gate_block(k, place_ref):
        return (0, column(k, place_ref))

    def up_block(k, place_ref):
        return (0, NY + column(k, place_ref))

    outs = [shaped(total // 2, 2 * part)] * 2 if first == 2 else [shaped(total, 2 * part)] * count
    return run(
        up_kernel,
        after,
        place,
        [own, other, w_gate, w_up, swapped, swapped],
        outs,
        [pltpu.VMEM((total, 2 * width), BF16)],
        (count,),
        [whole()] * 2
        + [pl.BlockSpec((1, width, part), own_block)] * 2
        + [pl.BlockSpec((width, part), gate_block), pl.BlockSpec((width, part), up_block)],
    )


def add_kernel(place_ref, plus_ref, minus_ref, far_plus, far_minus, out_plus, out_minus):
    half = far_plus.shape[0]
    out_plus[0:half] = (plus_ref[0:half].astype(F32) + far_plus[...].astype(F32)).astype(BF16)
    out_plus[half:] = plus_ref[half:]
    out_minus[0:half] = minus_ref[0:half]
    out_minus[half:] = (minus_ref[half:].astype(F32) + far_minus[...].astype(F32)).astype(BF16)


def pair_kernel(place_ref, a, b, c, d, first_ref, second_ref):
    first_ref[...] = (a[...].astype(F32) + b[...].astype(F32)).astype(BF16)
    second_ref[...] = (c[...].astype(F32) + d[...].astype(F32)).astype(BF16)


def act_kernel(place_ref, own, plus, minus, out_ref):
    total = own[...].astype(F32) + plus[...].astype(F32) + minus[...].astype(F32)
    part = out_ref.shape[1]
    out_ref[...] = (jax.nn.silu(total[:, 0:part]) * total[:, part : 2 * part]).astype(BF16)


def down_kernel(count, place_ref, *refs):
    actives, weight_refs, out_refs, held = (
        refs[: 2 * count],
        refs[2 * count : 2 * count + 2 * NY],
        refs[2 * count + 2 * NY : -1],
        refs[-1],
    )
    part = weight_refs[0].shape[1]
    for c in range(2):
        for i in range(count):
            block = actives[c * count + i]
            if i < NY - 1:
                held[:, (c * NY + i) * part : (c * NY + i + 1) * part] = block[...]
            else:
                half = block.shape[0]
                start = (i - NY + 1) * half
                held[start : start + half, (c * NY + NY - 1) * part : (c * NY + NY) * part] = block[...]
    weight = jnp.concatenate([w[0] for w in weight_refs], axis=0)
    result = jnp.dot(held[...], weight, preferred_element_type=F32).astype(BF16)
    start = 0
    for out_ref in out_refs:
        rows = out_ref.shape[0]
        out_ref[...] = result[start : start + rows, :]
        start += rows


def down_projection(parts, after, place, own, other, w_down):
    total, part = own[0].shape
    width = w_down.shape[2]

    def weight_block(distance, flip):
        def at(k, place_ref):
            core = 1 - place_ref[3] if flip else place_ref[3]
            return (0, core * NY + lax.rem(place_ref[2] + distance, NY), 0)

        return pl.BlockSpec((1, part, width), at)

    actives = list(own) + list(other)
    return run(
        functools.partial(down_kernel, len(own)),
        after,
        place,
        actives + [w_down] * (2 * NY),
        [shaped(rows, width) for _ in range(NX) for rows in parts],
        [pltpu.VMEM((total, 2 * NY * part), BF16)],
        None,
        [whole()] * len(actives)
        + [weight_block(d, flip) for flip in (False, True) for d in (0, NY - 1, 1, 2)],
    )


def total_of(*terms):
    return sum(t.astype(F32) for t in terms).astype(BF16)


def across_x(values, way):
    return [values[0]] + [shift(values[j], "x", NX, way * j) for j in range(1, NX)]


def per_device(moe_rows, expert_ids, route_weight, w_gate, w_up, w_down):
    place = jnp.stack([lax.axis_index(a) for a in ("z", "x", "y", "core")]).astype(jnp.int32)

    own = pack(moe_rows, expert_ids.T, route_weight.T)
    arrived = {0: (own,)}
    plus, minus = own, own
    for step in range(1, NZ // 2):
        plus, minus = shift(plus, "z", NZ, 1), shift(minus, "z", NZ, -1)
        arrived[-step], arrived[step] = (plus,), (minus,)
    last, swapped = other_half((WORK, []), place, w_gate, w_up)
    weights = (w_gate, w_up, swap(swapped))
    half = TOKENS // 2
    arrived[NZ // 2] = (
        shift(plus[:half], "z", NZ, 1),
        shift(minus[half:], "z", NZ, -1),
    )

    state = [{} for _ in CHUNKS]
    sums = {}
    for step, c in ORDER:
        chunk, s = (CHUNKS[c], state[c]) if step != "home" else (None, None)
        after = (WORKS.get((step, c), WORK), [last])
        if step == "pick":
            blocks = [b for offset in chunk for b in arrived[offset]]
            last, *outgoing, s["meta"] = pick(chunk, after, place, blocks)
            s["pieces"] = across_x(outgoing, 1)
        elif step == "join":
            rows, width = s["pieces"][0].shape
            last, s["own"] = run(join_kernel, after, place, s["pieces"], [shaped(NX * rows, width)])
            s["other"] = swap(s["own"])
        elif step == "far":
            last, top, bottom = up_projection(2, 1, after, place, s["own"], s["other"], weights)
            s["far"] = shift(top, "y", NY, 1), shift(bottom, "y", NY, -1)
        elif step == "near":
            last, s["minus"], s["plus"] = up_projection(3, 2, after, place, s["own"], s["other"], weights)
        elif step == "mine":
            last, s["mine"] = up_projection(0, 1, after, place, s["own"], s["other"], weights)
        elif step == "add":
            last, *near = run(
                add_kernel, after, place, [s["plus"], s["minus"], *s["far"]], [shaped(*s["plus"].shape)] * 2
            )
            s["near"] = shift(near[0], "y", NY, 1), shift(near[1], "y", NY, -1)
        elif step == "act":
            total, both = s["mine"].shape
            last, active = run(
                act_kernel, after, place, [s["mine"], *s["near"]], [shaped(total, both // 2)]
            )
            below, above = shift(active, "y", NY, 1), shift(active, "y", NY, -1)
            middle = total // 2
            s["active"] = [
                active,
                below,
                above,
                shift(below[:middle], "y", NY, 1),
                shift(above[middle:], "y", NY, -1),
            ]
        elif step == "down":
            parts = PARTS[c]
            last, *result = down_projection(
                parts, after, place, s["active"], [swap(a) for a in s["active"]], w_down
            )
            s["back"] = [across_x(result[k :: len(parts)], -1) for k in range(len(parts))]
        elif step in ("mix", "rest"):
            cut = len(chunk) if c else 2
            part, back = (range(cut), s["back"][:1]) if step == "mix" else (range(cut, len(chunk)), s["back"])
            last, *partial = mix(chunk, part, after, place, s["meta"], back)
            sums.update((chunk[i], partial[2 * n : 2 * n + 2]) for n, i in enumerate(part))
        elif step == "home":
            h, d = c % 2, 3 - c // 2
            if d == 3 and h == 0:
                moving = [
                    [shift(sums[4][0], "z", NZ, 1), shift(sums[4][1], "z", NZ, -1)],
                    [shift(sums[3][1], "z", NZ, 1), shift(sums[-3][0], "z", NZ, -1)],
                ]
            if d < 3 or h == 0:
                terms = [sums[d][h], moving[h][0], sums[-d][1 - h], moving[h][1]]
                last, up, down = run(pair_kernel, after, place, terms, [shaped(*t.shape) for t in terms[::2]])
                moving[h] = [shift(up, "z", NZ, 1), shift(down, "z", NZ, -1)]

    return jnp.concatenate([total_of(sums[0][h], moving[h][0], moving[1 - h][1]) for h in range(2)])


def solution(mesh):
    split = Mesh(mesh.devices.reshape(NY, 2, NZ, NX), ("y", "core", "z", "x"))
    exp, ctx = ("z", "x"), ("y", "core")
    return jax.shard_map(
        per_device,
        mesh=split,
        in_specs=(
            P(exp, ctx),
            P(exp, None),
            P(exp, None),
            P(exp, ctx, None),
            P(exp, ctx, None),
            P(exp, None, ctx),
        ),
        out_specs=P(exp, ctx),
        check_vma=False,
    )
```
